256 devices in a mesh: col: 32 (over x, y, core), row: 8 (over z).
Axes of the slice: x: 4, y: 4, z: 8, core: 2. Of those that a mesh axis runs over, the one named last changes fastest.
Arguments:
- w_tiles: bfloat16 [256, 512, 512], P(('col', 'row')), may hold values from -0.03125 to 0.03125
- task_ab: int32 [256], P(('col', 'row')), may hold values from 0 to 3, as said below
- task_ef: int32 [256], P(('col', 'row')), may hold values from 0 to 7
- lam_pairs: bfloat16 [32768, 16384], P('row', 'col'), may hold values from -6 to 6
- other_terms: bfloat16 [2048, 16384], P('row', 'col'), may hold values from -6 to 6
- vir_pair: float32 [2048], P('row'), may hold values from 1 to 4
- occ_pair: float32 [16384], P('col'), may hold values from -3 to -1
Outputs:
- lam_new: bfloat16 [2048, 16384], P('row', 'col')
The draws below stay inside these ranges and needn't reach their ends.
Inputs may be any that keep to these rules, and one draw needn't show every extreme that they name: Within one row group no pair (task_ab, task_ef) is listed twice.
All inputs are finite; a program needn't handle non-finite values.
Results may differ from the reference program's by a relative error of at most 0.001.
Values may be sent and summed in bfloat16 or wider, within the bound.
A program may use at most 64 MiB of HBM per device.

```python
import jax
import jax.numpy as jnp
from jax import lax

TILE = 512
AB_T = 4
EF_DEV_T = 8
TASK_DEV = 1
AB = 2048
EF = 32768
IJ = 16384
TASKS = 256
N_COL = 32
N_ROW = 8


def block_ids(key):
    block_total = AB_T * EF_DEV_T
    group_keys = jax.random.split(jax.random.fold_in(key, 7151), N_ROW)
    perms = jax.vmap(lambda k: jax.random.permutation(k, block_total))(group_keys).astype(jnp.int32)
    order = jnp.arange(TASKS, dtype=jnp.int32)
    device = order // TASK_DEV
    group = device % N_ROW
    within = device // N_ROW * TASK_DEV + order % TASK_DEV
    return perms[group, within].astype(jnp.int32)


def draw_task_ab(key, part):
    return (block_ids(key) // EF_DEV_T).astype(jnp.int32)


def draw_task_ef(key, part):
    return (block_ids(key) % EF_DEV_T).astype(jnp.int32)


def shard_levels(key, dims, cuts, low, largest):
    loudness, own = 1.0, jax.random.fold_in(key, 6)
    for position, blocks in cuts:
        steps = jnp.exp(jax.random.uniform(jax.random.fold_in(own, position), (blocks,), jnp.float32, low / len(cuts), largest / len(cuts)))
        loudness = loudness * jnp.repeat(steps, dims[position] // blocks).reshape([-1 if axis == position else 1 for axis in range(len(dims))])
    return loudness


def gaussian(rng, extent, scale, most, shards=(), kind=jnp.bfloat16):
    array = jax.random.normal(rng, extent, jnp.float32) * scale
    if len(shards) > 0:
        array = shard_levels(rng, extent, shards, -0.22, 0.18) * array
    return jnp.clip(array, min=-most, max=most).astype(kind)


def setup_inputs(seed: int = 0) -> dict:
    seeds = jax.random.split(jax.random.key(seed), 8)
    w_tiles = gaussian(seeds[0], (TASKS, TILE, TILE), (TILE * TASK_DEV * N_COL * N_ROW // AB_T) ** -0.5, 0.03125, ((0, 256),))
    task_ab = draw_task_ab(jax.random.fold_in(seeds[7], 71), 0)
    task_ef = draw_task_ef(jax.random.fold_in(seeds[7], 71), 0)
    lam_pairs = gaussian(seeds[3], (EF, IJ), 1.0, 6.0, ((0, 8), (1, 32)))
    other_terms = gaussian(seeds[4], (AB, IJ), 1.0, 6.0, ((0, 8), (1, 32)))
    vir_pair = jnp.clip(1.0 + 3.0 * jax.random.uniform(seeds[5], (AB,), jnp.float32) ** shard_levels(seeds[5], (AB,), ((0, 8),), -0.2, 0.2), 1.0, 4.0)
    occ_pair = jnp.clip(-3.0 + 2.0 * jax.random.uniform(seeds[6], (IJ,), jnp.float32) ** shard_levels(seeds[6], (IJ,), ((0, 32),), -0.2, 0.2), -3.0, -1.0)
    return {"w_tiles": w_tiles, "task_ab": task_ab, "task_ef": task_ef, "lam_pairs": lam_pairs, "other_terms": other_terms, "vir_pair": vir_pair, "occ_pair": occ_pair}


def reference(w_tiles, task_ab, task_ef, lam_pairs, other_terms, vir_pair, occ_pair):
    col_count = lam_pairs.shape[1]
    lam_blocks = lam_pairs.astype(jnp.float32).reshape(N_ROW * EF_DEV_T, TILE, col_count)
    order = jnp.arange(TASKS, dtype=jnp.int32)
    group = (order // TASK_DEV) % N_ROW
    ef_tile = (group * EF_DEV_T + task_ef).astype(jnp.int32)

    def step(totals, items):
        tile_now, ab_id, ef_id = items
        block = lax.dynamic_index_in_dim(lam_blocks, ef_id, 0, keepdims=False)
        product = jnp.dot(tile_now.astype(jnp.float32), block, precision=lax.Precision.HIGHEST)
        totals = totals.at[ab_id].add(product)
        return totals, None

    start = jnp.zeros((AB_T, TILE, col_count), jnp.float32)
    totals, unused = lax.scan(step, start, (w_tiles, task_ab.astype(jnp.int32), ef_tile))
    ladder = totals.reshape(AB_T * TILE, col_count)
    combined = other_terms.astype(jnp.float32) + ladder
    denominator = occ_pair[None, :] - vir_pair[:, None]
    return (combined / denominator).astype(jnp.bfloat16)
```

```python
import jax
import jax.numpy as jnp
from jax import lax
from jax.experimental import pallas as pl
from jax.experimental.pallas import tpu as pltpu
from jax.sharding import PartitionSpec as P

TILE = 512
AB_T = 4
EF_T = 8
NX = NY = 4
NZ = 8
NK = 8
R = 16
W2 = 512

S_1A, S_1B, S_2A, S_2B, S_MM, S_H1, S_H2, S_H3, S_FIN = range(9)


def kernel(ab_ref, ef_ref, w_ref, lam_ref, other_ref, vir_ref, occ_ref, out_ref, *scratch):
    land = scratch[:NK]
    part = scratch[NK : 2 * NK]
    (
        lam_v, lhs, hop0, hop1, hop2, last, swap, other_v, vir_v, occ_v, vir_t,
        ids, inv_v, inv_s,
        in_sem, start_send, start_recv, id_send, id_recv, g_send, g_recv,
        h_send, h_recv, l_send, l_recv, s_send, s_recv,
    ) = scratch[2 * NK :]

    col = lax.axis_index("col")
    z = lax.axis_index("row")
    core = lax.rem(col, 2)
    y = lax.rem(col // 2, NY)
    x = col // (2 * NY)

    def dev(xx, yy, cc, zz):
        return ((xx * NY + yy) * 2 + cc, zz)

    def step4(v, d):
        return lax.rem(v + (4 + d), 4)

    def stepz(v, d):
        return lax.rem(v + (NZ + d), NZ)

    def remote(src, dst, send, recv, device):
        return pltpu.make_async_remote_copy(
            src_ref=src, dst_ref=dst, send_sem=send, recv_sem=recv,
            device_id=device, device_id_type=pl.DeviceIdType.MESH,
        )

    partner = dev(x, y, 1 - core, z)
    prime = (x, y)
    second = (y, x)
    around1 = (
        {d: dev(step4(x, d), y, core, z) for d in (1, -1)},
        {d: dev(x, step4(y, d), core, z) for d in (1, -1)},
    )
    around2 = (around1[1], around1[0])
    updown = {d: [dev(x, y, j, stepz(z, d)) for j in (0, 1)] for d in (1, -1)}
    updown_same = {d: dev(x, y, core, stepz(z, d)) for d in (1, -1)}

    def slot(g, s, p):
        return g * 16 + s * 4 + p

    my_slot = core * 16 + jnp.where(core == 0, y * 4 + x, x * 4 + y)

    barrier = pltpu.get_barrier_semaphore()
    greeted = [partner]
    for d in (1, -1):
        greeted += [around1[0][d], around1[1][d], updown[d][0], updown[d][1]]
    for who in greeted:
        pl.semaphore_signal(barrier, inc=1, device_id=who, device_id_type=pl.DeviceIdType.MESH)

    local_w = [
        pltpu.make_async_copy(w_ref.at[:, core, k], land[k].at[my_slot], in_sem.at[k])
        for k in range(NK)
    ]
    for c in local_w:
        c.start()
    local_lam = pltpu.make_async_copy(lam_ref, lam_v.at[core], in_sem.at[NK])
    local_lam.start()
    small = [
        pltpu.make_async_copy(vir_ref, vir_v, in_sem.at[NK + 1]),
        pltpu.make_async_copy(occ_ref, occ_v, in_sem.at[NK + 2]),
        pltpu.make_async_copy(other_ref, other_v, in_sem.at[NK + 3]),
    ]
    for c in small:
        c.start()

    code = ab_ref[0] * EF_T + ef_ref[0]
    lane = lax.broadcasted_iota(jnp.int32, (8, 128), 1)
    ids[y, x, core] = jnp.where(lane == code, my_slot, 0)

    pl.semaphore_wait(barrier, len(greeted))

    sent = []

    def go(copy):
        copy.start()
        sent.append(copy)
        return copy

    start_w = [
        go(remote(w_ref.at[:, 1 - core, k], land[k].at[my_slot], start_send.at[k], start_recv.at[k], partner))
        for k in range(NK)
    ]
    id0 = go(remote(ids.at[y, x, core], ids.at[y, x, core], id_send.at[0], id_recv.at[0], partner))
    start_lam = go(remote(lam_ref, lam_v.at[core], start_send.at[NK], start_recv.at[NK], partner))

    moves = {}

    def gather_copy(k, g, stage, d):
        s, p = second[g], prime[g]
        ref = land[k]
        n = 0 if d == 1 else 1
        if stage == 0:
            view, who = ref.at[slot(g, s, p)], around1[g][d]
        elif stage == 1:
            view, who = ref.at[slot(g, s, step4(p, -d)), n], around1[g][d]
        elif stage == 2:
            view, who = ref.at[pl.ds(slot(g, s, 0), 4)], around2[g][d]
        else:
            view, who = ref.at[pl.ds(slot(g, step4(s, -d), 2 * n), 2)], around2[g][d]
        moves[k, g, stage, d] = go(
            remote(view, view, g_send.at[k, g, stage, n], g_recv.at[k, g, stage, n], who)
        )

    def stage_1a(k):
        local_w[k].wait()
        start_w[k].wait_recv()
        for g in (0, 1):
            for d in (1, -1):
                gather_copy(k, g, 0, d)

    def stage_next(k, stage):
        for g in (0, 1):
            for d in (1, -1):
                moves[k, g, stage - 1, d].wait_recv()
                if stage in (1, 3):
                    gather_copy(k, g, stage, d)
            if stage == 2:
                for d in (1, -1):
                    gather_copy(k, g, stage, d)

    id_moves = {}

    def id_copy(n, view, who):
        id_moves[n] = go(remote(view, view, id_send.at[n], id_recv.at[n], who))

    def id_stage(s):
        if s == 0:
            id0.wait_recv()
            id_copy(1, ids.at[y, x], around1[0][1])
            id_copy(2, ids.at[y, x], around1[0][-1])
        elif s == 1:
            id_moves[1].wait_recv()
            id_copy(3, ids.at[y, step4(x, -1)], around1[0][1])
            id_moves[2].wait_recv()
        elif s == 2:
            id_moves[3].wait_recv()
            id_copy(4, ids.at[y], around1[1][1])
            id_copy(5, ids.at[y], around1[1][-1])
        elif s == 3:
            id_moves[4].wait_recv()
            id_copy(6, ids.at[step4(y, -1)], around1[1][1])
            id_moves[5].wait_recv()
        else:
            id_moves[6].wait_recv()
            inv_v[...] = jnp.max(ids[...], axis=(0, 1, 2))
            get = pltpu.make_async_copy(inv_v, inv_s, in_sem.at[NK + 4])
            get.start()
            for c in small:
                c.wait()
            for n in (0, 1):
                row = jnp.broadcast_to(vir_v[n : n + 1, :], (128, 128))
                vir_t[n * 128 : (n + 1) * 128, :] = row.T
            get.wait()
            local_lam.wait()
            start_lam.wait_recv()

    def multiply(k):
        for g in (0, 1):
            for d in (1, -1):
                moves[k, g, 3, d].wait_recv()

        def order(ab, carry):
            for ef in range(EF_T):
                tile = land[k][inv_s[0, ab * EF_T + ef]]
                lhs[pl.ds(pl.multiple_of(ab * (2 * R), 2 * R), 2 * R), ef * TILE : (ef + 1) * TILE] = tile.reshape(2 * R, TILE)
            return carry

        lax.fori_loop(0, AB_T, order, 0)

        def half(j, carry):
            for q in range(W2 // 256):
                cols = slice(q * 256, (q + 1) * 256)
                product = jnp.dot(lhs[...], lam_v[j, :, cols], preferred_element_type=jnp.float32)
                part[k][j, :, :, cols] = product.reshape(NZ, R, 256)
            return carry

        lax.fori_loop(0, 2, half, 0)
        far = stepz(z, 4)
        for n, d in enumerate((1, -1)):
            moves[k, "h0", d] = go(
                remote(part[k].at[n, far], hop0.at[k, n], h_send.at[k, 0, n], h_recv.at[k, 0, n], updown_same[d])
            )
        moves[k, "swap"] = go(
            remote(part[k].at[1 - core, z], swap.at[k], s_send.at[k], s_recv.at[k], partner)
        )

    def hop_1(k):
        for n, d in enumerate((1, -1)):
            moves[k, "h0", d].wait_recv()
            block = stepz(z, 3 * d)
            part[k][n, block] = part[k][n, block] + hop0[k, n]
            moves[k, "h1", d] = go(
                remote(part[k].at[:, block], hop1.at[k, n], h_send.at[k, 1, n], h_recv.at[k, 1, n], updown_same[d])
            )

    def hop_2(k):
        for n, d in enumerate((1, -1)):
            moves[k, "h1", d].wait_recv()
            block = stepz(z, 2 * d)
            part[k][:, block] = part[k][:, block] + hop1[k, n]
            moves[k, "h2", d] = go(
                remote(part[k].at[:, block], hop2.at[k, n], h_send.at[k, 2, n], h_recv.at[k, 2, n], updown_same[d])
            )

    def hop_3(k):
        for n, d in enumerate((1, -1)):
            moves[k, "h2", d].wait_recv()
            block = stepz(z, d)
            for j in (0, 1):
                part[k][j, block] = part[k][j, block] + hop2[k, n, j]
                moves[k, "h3", d, j] = go(
                    remote(
                        part[k].at[j, block], last.at[k, n, core],
                        l_send.at[k, n, j], l_recv.at[k, n, core], updown[d][j],
                    )
                )

    def finish(k):
        moves[k, "swap"].wait_recv()
        for n in (0, 1):
            for j in (0, 1):
                here = last.at[k, n, j]
                remote(here, here, l_send.at[k, n, j], l_recv.at[k, n, j], partner).wait_recv()
        for who, own in ((core, part[k][core, z]), (1 - core, swap[k])):
            rows = pl.ds(pl.multiple_of(who * 128 + k * R, R), R)
            ladder = own + last[k, 0, who] + last[k, 1, who]
            v = vir_t[rows, :]
            den = occ_v[...] - jnp.concatenate([v] * (W2 // 128), axis=1)
            out_ref[rows, :] = ((other_v[rows, :].astype(jnp.float32) + ladder) / den).astype(jnp.bfloat16)

    for step in range(NK + S_FIN):
        def at(offset):
            k = step - offset
            return k if 0 <= k < NK else None

        k = at(S_1A)
        if k is not None:
            stage_1a(k)
        if step <= 4:
            id_stage(step)
        for offset, stage in ((S_1B, 1), (S_2A, 2), (S_2B, 3)):
            k = at(offset)
            if k is not None:
                stage_next(k, stage)
        for offset, run in ((S_MM, multiply), (S_H1, hop_1), (S_H2, hop_2), (S_H3, hop_3), (S_FIN, finish)):
            k = at(offset)
            if k is not None:
                run(k)

    for c in sent:
        c.wait_send()


def body(w_tiles, task_ab, task_ef, lam_pairs, other_terms, vir_pair, occ_pair):
    w = w_tiles.reshape(2, 2, NK, R, TILE)
    anyspace = pl.BlockSpec(memory_space=pl.ANY)
    smem = pl.BlockSpec(memory_space=pltpu.SMEM)
    f32, bf16 = jnp.float32, jnp.bfloat16
    dma = pltpu.SemaphoreType.DMA
    scratch = [pltpu.VMEM((32, 2, R, TILE), bf16) for _ in range(NK)]
    scratch += [pltpu.VMEM((2, NZ, R, W2), f32) for _ in range(NK)]
    scratch += [
        pltpu.VMEM((2, EF_T * TILE, W2), bf16),
        pltpu.VMEM((AB_T * 2 * R, EF_T * TILE), bf16),
        pltpu.VMEM((NK, 2, R, W2), f32),
        pltpu.VMEM((NK, 2, 2, R, W2), f32),
        pltpu.VMEM((NK, 2, 2, R, W2), f32),
        pltpu.VMEM((NK, 2, 2, R, W2), f32),
        pltpu.VMEM((NK, R, W2), f32),
        pltpu.VMEM((256, W2), bf16),
        pltpu.VMEM((2, 128), f32),
        pltpu.VMEM((1, W2), f32),
        pltpu.VMEM((256, 128), f32),
        pltpu.VMEM((NY, NX, 2, 8, 128), jnp.int32),
        pltpu.VMEM((8, 128), jnp.int32),
        pltpu.SMEM((8, 128), jnp.int32),
        dma((NK + 5,)),
        dma((NK + 1,)), dma((NK + 1,)),
        dma((7,)), dma((7,)),
        dma((NK, 2, 4, 2)), dma((NK, 2, 4, 2)),
        dma((NK, 3, 2)), dma((NK, 3, 2)),
        dma((NK, 2, 2)), dma((NK, 2, 2)),
        dma((NK,)), dma((NK,)),
    ]
    return pl.pallas_call(
        kernel,
        out_shape=jax.ShapeDtypeStruct((256, W2), bf16),
        in_specs=[smem, smem] + [anyspace] * 5,
        out_specs=pl.BlockSpec(memory_space=pltpu.VMEM),
        scratch_shapes=scratch,
        compiler_params=pltpu.CompilerParams(
            collective_id=0, has_side_effects=True, vmem_limit_bytes=48 * 1024 * 1024
        ),
        cost_estimate=pl.CostEstimate(
            flops=2 * 2048 * 4096 * 512, bytes_accessed=6 * 1024 * 1024, transcendentals=0
        ),
    )(task_ab, task_ef, w, lam_pairs, other_terms, vir_pair.reshape(2, 128), occ_pair.reshape(1, W2))


def solution(mesh):
    placed = (
        P(("col", "row"), None, None),
        P(("col", "row")),
        P(("col", "row")),
        P("row", "col"),
        P("row", "col"),
        P("row"),
        P("col"),
    )
    return jax.shard_map(
        body, mesh=mesh, in_specs=placed, out_specs=P("row", "col"), check_vma=False
    )
```

```python
import jax
import jax.numpy as jnp
from jax import lax
from jax.experimental import pallas as pl
from jax.experimental.pallas import tpu as pltpu
from jax.sharding import PartitionSpec as P

TILE = 512
AB_T = 4
EF_T = 8
NX = NY = 4
NZ = 8
NK = 8
R = 16
W2 = 512
VMEM = 63 * 1024 * 1024

S_1A, S_1B, S_2A, S_2B, S_MM, S_H1, S_H2, S_H3, S_FIN = range(9)


def timetable():
    table = {}

    def put(step, stage, k):
        table.setdefault((step, stage), []).append(k)

    for k in range(NK):
        if k == 0:
            times = {S_1A: 0, S_2A: 1, S_MM: 2, S_H1: 3, S_H2: 4, S_H3: 5, S_FIN: 6}
        else:
            times = {stage: k - 1 + stage for stage in range(9)}
        for stage, step in times.items():
            put(step, stage, k)
    return table


def kernel(ab_ref, ef_ref, w_ref, lam_ref, other_ref, vir_ref, occ_ref, out_ref, *scratch):
    land = scratch[:NK]
    part = scratch[NK : 2 * NK]
    (
        w_v, lam_v, lhs, hop0, hop1, hop2, last, swap, other_v, vir_v, occ_v, vir_t,
        ids, inv_v, inv_s,
        in_sem, lam_send, lam_recv, id_send, id_recv, g_send, g_recv,
        h_send, h_recv, s_send, s_recv,
    ) = scratch[2 * NK :]

    col = lax.axis_index("col")
    z = lax.axis_index("row")
    core = lax.rem(col, 2)
    y = lax.rem(col // 2, NY)
    x = col // (2 * NY)

    def dev(xx, yy, cc, zz):
        return ((xx * NY + yy) * 2 + cc, zz)

    def step4(v, d):
        return lax.rem(v + (4 + d), 4)

    def stepz(v, d):
        return lax.rem(v + (NZ + d), NZ)

    def remote(src, dst, send, recv, device):
        return pltpu.make_async_remote_copy(
            src_ref=src, dst_ref=dst, send_sem=send, recv_sem=recv,
            device_id=device, device_id_type=pl.DeviceIdType.MESH,
        )

    partner = dev(x, y, 1 - core, z)
    prime = (x, y)
    second = (y, x)
    near = {
        (axis, d, j): dev(step4(x, d), y, j, z) if axis == 0 else dev(x, step4(y, d), j, z)
        for axis in (0, 1) for d in (1, -1, 2) for j in (0, 1)
    }

    def around(axis, d, j):
        if axis == 0:
            return dev(step4(x, d), y, j, z)
        return dev(x, step4(y, d), j, z)

    updown = {d: [dev(x, y, j, stepz(z, d)) for j in (0, 1)] for d in (1, -1)}

    get_w = pltpu.make_async_copy(w_ref, w_v, in_sem.at[0])
    get_w.start()
    get_lam = pltpu.make_async_copy(lam_ref, lam_v.at[core], in_sem.at[1])
    get_lam.start()
    small = [
        pltpu.make_async_copy(vir_ref, vir_v, in_sem.at[2]),
        pltpu.make_async_copy(occ_ref, occ_v, in_sem.at[3]),
        pltpu.make_async_copy(other_ref, other_v, in_sem.at[4]),
    ]
    for c in small:
        c.start()

    barrier = pltpu.get_barrier_semaphore()
    greeted = [partner] + list(near.values()) + updown[1] + updown[-1]
    for who in greeted:
        pl.semaphore_signal(barrier, inc=1, device_id=who, device_id_type=pl.DeviceIdType.MESH)

    my_slot = core * 16 + jnp.where(core == 0, y * 4 + x, x * 4 + y)
    my_id = (y * 4 + x) * 2 + core
    code = ab_ref[0] * EF_T + ef_ref[0]
    lane = lax.broadcasted_iota(jnp.int32, (8, 128), 1)
    ids[my_id] = jnp.where(lane == code, my_slot, 0)
    get_w.wait()
    for k in range(NK):
        land[k][my_slot] = w_v[:, core, k]

    pl.semaphore_wait(barrier, len(greeted))

    sent = []

    def mine_along(d, j):
        xx = jnp.where(core == 0, step4(x, d), x)
        yy = jnp.where(core == 0, y, step4(y, d))
        return dev(xx, yy, j, z)

    def stage_1a(k):
        send, recv = g_send.at[k, 0], g_recv.at[k, 0]
        hops = (1, -1, 2) if k == 0 else (1, -1)
        for d in hops:
            for j in (0, 1):
                remote(w_v.at[:, j, k], land[k].at[my_slot], send, recv, mine_along(d, j)).start()
        remote(w_v.at[:, 1 - core, k], land[k].at[my_slot], send, recv, partner).start()
        expect(land[k].at[pl.ds(0, 2 * len(hops) + 1)], send, recv, (k, 0))

    arrivals = {}

    def expect(view, send, recv, key):
        both = remote(view, view, send, recv, partner)
        arrivals[key] = both
        sent.append(both)

    def slot(g, s, p):
        return g * 16 + s * 4 + p

    def stage_1b(k):
        arrivals[k, 0].wait_recv()
        send, recv = g_send.at[k, 1], g_recv.at[k, 1]
        for g in (0, 1):
            for n, d in enumerate((1, -1)):
                view = land[k].at[slot(g, second[g], step4(prime[g], -d)), n]
                remote(view, view, send, recv, around(g, d, core)).start()
        expect(land[k].at[pl.ds(0, 2)], send, recv, (k, 1))

    def stage_2a(k):
        arrivals[k, 0 if k == 0 else 1].wait_recv()
        send, recv = g_send.at[k, 2], g_recv.at[k, 2]
        hops = (1, -1, 2) if k == 0 else (1, -1)
        for g in (0, 1):
            view = land[k].at[pl.ds(slot(g, second[g], 0), 4)]
            for d in hops:
                remote(view, view, send, recv, around(1 - g, d, core)).start()
        expect(land[k].at[pl.ds(0, 8 * len(hops))], send, recv, (k, 2))

    def stage_2b(k):
        arrivals[k, 2].wait_recv()
        send, recv = g_send.at[k, 3], g_recv.at[k, 3]
        for g in (0, 1):
            for n, d in enumerate((1, -1)):
                view = land[k].at[pl.ds(slot(g, step4(second[g], -d), 2 * n), 2)]
                remote(view, view, send, recv, around(1 - g, d, core)).start()
        expect(land[k].at[pl.ds(0, 8)], send, recv, (k, 3))

    def ids_first():
        for d in (1, -1, 2):
            for j in (0, 1):
                remote(ids.at[my_id], ids.at[my_id], id_send.at[0], id_recv.at[0], around(0, d, j)).start()
        remote(ids.at[my_id], ids.at[my_id], id_send.at[0], id_recv.at[0], partner).start()
        expect(ids.at[pl.ds(0, 7)], id_send.at[0], id_recv.at[0], "id0")

    def ids_second():
        arrivals["id0"].wait_recv()
        view = ids.at[pl.ds(y * 8, 8)]
        for d in (1, -1, 2):
            remote(view, view, id_send.at[1], id_recv.at[1], around(1, d, core)).start()
        expect(ids.at[pl.ds(0, 24)], id_send.at[1], id_recv.at[1], "id1")

    def ids_done():
        arrivals["id1"].wait_recv()
        inv_v[...] = jnp.max(ids[...], axis=0)
        get = pltpu.make_async_copy(inv_v, inv_s, in_sem.at[5])
        get.start()
        for c in small:
            c.wait()
        for n in (0, 1):
            row = jnp.broadcast_to(vir_v[n : n + 1, :], (128, 128))
            vir_t[n * 128 : (n + 1) * 128, :] = row.T
        get.wait()
        get_lam.wait()
        give_lam.wait_recv()

    def multiply(k):
        arrivals[k, 2 if k == 0 else 3].wait_recv()

        def order(ab, carry):
            for ef in range(EF_T):
                tile = land[k][inv_s[0, ab * EF_T + ef]]
                rows = pl.ds(pl.multiple_of(ab * (2 * R), 2 * R), 2 * R)
                lhs[rows, ef * TILE : (ef + 1) * TILE] = tile.reshape(2 * R, TILE)
            return carry

        lax.fori_loop(0, AB_T, order, 0)

        def half(j, carry):
            for q in range(W2 // 256):
                cols = slice(q * 256, (q + 1) * 256)
                product = jnp.dot(lhs[...], lam_v[j, :, cols], preferred_element_type=jnp.float32)
                part[k][j, :, :, cols] = product.reshape(NZ, R, 256)
            return carry

        lax.fori_loop(0, 2, half, 0)
        far = stepz(z, 4)
        send, recv = h_send.at[k, 0], h_recv.at[k, 0]
        for n, d in enumerate((1, -1)):
            remote(part[k].at[n, far], hop0.at[k, n], send, recv, near_z(d)).start()
        expect(hop0.at[k], send, recv, (k, "h0"))
        give = remote(part[k].at[1 - core, z], swap.at[k], s_send.at[k], s_recv.at[k], partner)
        give.start()
        arrivals[k, "swap"] = give
        sent.append(give)

    def near_z(d):
        return dev(x, y, core, stepz(z, d))

    def hop_1(k):
        arrivals[k, "h0"].wait_recv()
        send, recv = h_send.at[k, 1], h_recv.at[k, 1]
        for n, d in enumerate((1, -1)):
            block = stepz(z, 3 * d)
            part[k][n, block] = part[k][n, block] + hop0[k, n]
            remote(part[k].at[:, block], hop1.at[k, n], send, recv, near_z(d)).start()
        expect(hop1.at[k], send, recv, (k, "h1"))

    def hop_2(k):
        arrivals[k, "h1"].wait_recv()
        send, recv = h_send.at[k, 2], h_recv.at[k, 2]
        for n, d in enumerate((1, -1)):
            block = stepz(z, 2 * d)
            part[k][:, block] = part[k][:, block] + hop1[k, n]
            remote(part[k].at[:, block], hop2.at[k, n], send, recv, near_z(d)).start()
        expect(hop2.at[k], send, recv, (k, "h2"))

    def hop_3(k):
        arrivals[k, "h2"].wait_recv()
        send, recv = h_send.at[k, 3], h_recv.at[k, 3]
        for n, d in enumerate((1, -1)):
            block = stepz(z, d)
            for j in (0, 1):
                part[k][j, block] = part[k][j, block] + hop2[k, n, j]
                remote(part[k].at[j, block], last.at[k, n, core], send, recv, updown[d][j]).start()
        expect(last.at[k], send, recv, (k, "h3"))

    def finish(k):
        arrivals[k, "swap"].wait_recv()
        arrivals[k, "h3"].wait_recv()
        for who, own in ((core, part[k][core, z]), (1 - core, swap[k])):
            rows = pl.ds(pl.multiple_of(who * 128 + k * R, R), R)
            ladder = own + last[k, 0, who] + last[k, 1, who]
            v = vir_t[rows, :]
            den = occ_v[...] - jnp.concatenate([v] * (W2 // 128), axis=1)
            out_ref[rows, :] = ((other_v[rows, :].astype(jnp.float32) + ladder) / den).astype(jnp.bfloat16)

    stage_1a(0)
    ids_first()
    give_lam = remote(lam_ref, lam_v.at[core], lam_send, lam_recv, partner)
    give_lam.start()
    sent.append(give_lam)

    run = (stage_1a, stage_1b, stage_2a, stage_2b, multiply, hop_1, hop_2, hop_3, finish)
    table = timetable()
    for step in range(1 + max(step for step, stage in table)):
        if step == 1:
            ids_second()
        for stage in range(9):
            if step == 2 and stage == S_MM:
                ids_done()
            for k in table.get((step, stage), ()):
                if (k, stage) != (0, S_1A):
                    run[stage](k)

    for c in sent:
        c.wait_send()


def body(w_tiles, task_ab, task_ef, lam_pairs, other_terms, vir_pair, occ_pair):
    w = w_tiles.reshape(2, 2, NK, R, TILE)
    anyspace = pl.BlockSpec(memory_space=pl.ANY)
    smem = pl.BlockSpec(memory_space=pltpu.SMEM)
    f32, bf16 = jnp.float32, jnp.bfloat16
    dma = pltpu.SemaphoreType.DMA
    scratch = [pltpu.VMEM((32, 2, R, TILE), bf16) for _ in range(NK)]
    scratch += [pltpu.VMEM((2, NZ, R, W2), f32) for _ in range(NK)]
    scratch += [
        pltpu.VMEM((2, 2, NK, R, TILE), bf16),
        pltpu.VMEM((2, EF_T * TILE, W2), bf16),
        pltpu.VMEM((AB_T * 2 * R, EF_T * TILE), bf16),
        pltpu.VMEM((NK, 2, R, W2), f32),
        pltpu.VMEM((NK, 2, 2, R, W2), f32),
        pltpu.VMEM((NK, 2, 2, R, W2), f32),
        pltpu.VMEM((NK, 2, 2, R, W2), f32),
        pltpu.VMEM((NK, R, W2), f32),
        pltpu.VMEM((256, W2), bf16),
        pltpu.VMEM((2, 128), f32),
        pltpu.VMEM((1, W2), f32),
        pltpu.VMEM((256, 128), f32),
        pltpu.VMEM((32, 8, 128), jnp.int32),
        pltpu.VMEM((8, 128), jnp.int32),
        pltpu.SMEM((8, 128), jnp.int32),
        dma((6,)),
        dma, dma,
        dma((2,)), dma((2,)),
        dma((NK, 4)), dma((NK, 4)),
        dma((NK, 4)), dma((NK, 4)),
        dma((NK,)), dma((NK,)),
    ]
    return pl.pallas_call(
        kernel,
        out_shape=jax.ShapeDtypeStruct((256, W2), bf16),
        in_specs=[smem, smem] + [anyspace] * 5,
        out_specs=pl.BlockSpec(memory_space=pltpu.VMEM),
        scratch_shapes=scratch,
        compiler_params=pltpu.CompilerParams(
            collective_id=0, has_side_effects=True, vmem_limit_bytes=VMEM
        ),
        cost_estimate=pl.CostEstimate(
            flops=2 * 2048 * 4096 * 512, bytes_accessed=6 * 1024 * 1024, transcendentals=0
        ),
    )(task_ab, task_ef, w, lam_pairs, other_terms, vir_pair.reshape(2, 128), occ_pair.reshape(1, W2))


def solution(mesh):
    placed = (
        P(("col", "row"), None, None),
        P(("col", "row")),
        P(("col", "row")),
        P("row", "col"),
        P("row", "col"),
        P("row"),
        P("col"),
    )
    return jax.shard_map(
        body, mesh=mesh, in_specs=placed, out_specs=P("row", "col"), check_vma=False
    )
```

```python
import jax
import jax.numpy as jnp
from jax import lax
from jax.experimental import pallas as pl
from jax.experimental.pallas import tpu as pltpu
from jax.sharding import PartitionSpec as P

TILE = 512
AB_T = 4
EF_T = 8
NX = NY = 4
NZ = 8
NK = 8
R = 16
W2 = 512
VMEM = 63 * 1024 * 1024

S_1A, S_1B, S_2A, S_2B, S_MM, S_H1, S_H2, S_H3, S_FIN = range(9)


ORDER = (
     2,  0,  1,  4,  5, 12,  6,  3, 11, 10, 14, 22, 20, 32, 21, 24,
    30, 42,  7, 15, 31, 52, 13, 34, 16, 40, 25, 62, 41, 17, 23, 44,
    50, 51, 35, 26, 54, 27, 72, 61, 45, 60, 33, 36, 64, 71, 37, 55,
    70, 43, 74, 46, 47, 65, 81, 53, 56, 57, 75, 63, 66, 67, 82, 73,
    80, 76, 77, 83, 86, 84, 85, 87,
)
DIRECT = ()


def kernel(ab_ref, ef_ref, w_ref, lam_ref, other_ref, vir_ref, occ_ref, out_ref, *scratch):
    land = scratch[:NK]
    part = scratch[NK : 2 * NK]
    (
        w_v, lam_v, lhs, hop0, hop1, hop2, last, swap, other_v, vir_v, occ_v, vir_t,
        ids, inv_v, inv_s,
        in_sem, lam_send, lam_recv, id_send, id_recv, g_send, g_recv,
        h_send, h_recv, s_send, s_recv,
    ) = scratch[2 * NK :]

    col = lax.axis_index("col")
    z = lax.axis_index("row")
    core = lax.rem(col, 2)
    y = lax.rem(col // 2, NY)
    x = col // (2 * NY)

    def dev(xx, yy, cc, zz):
        return ((xx * NY + yy) * 2 + cc, zz)

    def step4(v, d):
        return lax.rem(v + (4 + d), 4)

    def stepz(v, d):
        return lax.rem(v + (NZ + d), NZ)

    def remote(src, dst, send, recv, device):
        return pltpu.make_async_remote_copy(
            src_ref=src, dst_ref=dst, send_sem=send, recv_sem=recv,
            device_id=device, device_id_type=pl.DeviceIdType.MESH,
        )

    partner = dev(x, y, 1 - core, z)
    prime = (x, y)
    second = (y, x)
    near = {
        (axis, d, j): dev(step4(x, d), y, j, z) if axis == 0 else dev(x, step4(y, d), j, z)
        for axis in (0, 1) for d in (1, -1, 2) for j in (0, 1)
    }

    def around(axis, d, j):
        if axis == 0:
            return dev(step4(x, d), y, j, z)
        return dev(x, step4(y, d), j, z)

    updown = {d: [dev(x, y, j, stepz(z, d)) for j in (0, 1)] for d in (1, -1)}

    get_w = pltpu.make_async_copy(w_ref, w_v, in_sem.at[0])
    get_w.start()
    get_lam = pltpu.make_async_copy(lam_ref, lam_v.at[core], in_sem.at[1])
    get_lam.start()
    small = [
        pltpu.make_async_copy(vir_ref, vir_v, in_sem.at[2]),
        pltpu.make_async_copy(occ_ref, occ_v, in_sem.at[3]),
        pltpu.make_async_copy(other_ref, other_v, in_sem.at[4]),
    ]
    for c in small:
        c.start()

    barrier = pltpu.get_barrier_semaphore()
    greeted = [partner] + list(near.values()) + updown[1] + updown[-1]
    for who in greeted:
        pl.semaphore_signal(barrier, inc=1, device_id=who, device_id_type=pl.DeviceIdType.MESH)

    my_slot = core * 16 + jnp.where(core == 0, y * 4 + x, x * 4 + y)
    my_id = (y * 4 + x) * 2 + core
    code = ab_ref[0] * EF_T + ef_ref[0]
    lane = lax.broadcasted_iota(jnp.int32, (1, 128), 1)
    ids[my_id] = jnp.where(lane == code, my_slot, 0)
    get_w.wait()
    for k in range(NK):
        land[k][my_slot] = w_v[:, core, k]

    pl.semaphore_wait(barrier, len(greeted))

    sent = []

    def mine_along(d, j):
        xx = jnp.where(core == 0, step4(x, d), x)
        yy = jnp.where(core == 0, y, step4(y, d))
        return dev(xx, yy, j, z)

    def stage_1a(k):
        send, recv = g_send.at[k, 0], g_recv.at[k, 0]
        hops = (1, -1, 2) if k in DIRECT else (1, -1)
        for d in hops:
            for j in (0, 1):
                remote(w_v.at[:, j, k], land[k].at[my_slot], send, recv, mine_along(d, j)).start()
        remote(w_v.at[:, 1 - core, k], land[k].at[my_slot], send, recv, partner).start()
        expect(land[k].at[pl.ds(0, 2 * len(hops) + 1)], send, recv, (k, 0))

    arrivals = {}

    def expect(view, send, recv, key):
        both = remote(view, view, send, recv, partner)
        arrivals[key] = both
        sent.append(both)

    def slot(g, s, p):
        return g * 16 + s * 4 + p

    def stage_1b(k):
        arrivals[k, 0].wait_recv()
        send, recv = g_send.at[k, 1], g_recv.at[k, 1]
        for g in (0, 1):
            for n, d in enumerate((1, -1)):
                view = land[k].at[slot(g, second[g], step4(prime[g], -d)), n]
                remote(view, view, send, recv, around(g, d, core)).start()
        expect(land[k].at[pl.ds(0, 2)], send, recv, (k, 1))

    def stage_2a(k):
        arrivals[k, 0 if k in DIRECT else 1].wait_recv()
        send, recv = g_send.at[k, 2], g_recv.at[k, 2]
        hops = (1, -1, 2) if k in DIRECT else (1, -1)
        for g in (0, 1):
            view = land[k].at[pl.ds(slot(g, second[g], 0), 4)]
            for d in hops:
                remote(view, view, send, recv, around(1 - g, d, core)).start()
        expect(land[k].at[pl.ds(0, 8 * len(hops))], send, recv, (k, 2))

    def stage_2b(k):
        arrivals[k, 2].wait_recv()
        send, recv = g_send.at[k, 3], g_recv.at[k, 3]
        for g in (0, 1):
            for n, d in enumerate((1, -1)):
                view = land[k].at[pl.ds(slot(g, step4(second[g], -d), 2 * n), 2)]
                remote(view, view, send, recv, around(1 - g, d, core)).start()
        expect(land[k].at[pl.ds(0, 8)], send, recv, (k, 3))

    def ids_first():
        for d in (1, -1, 2):
            for j in (0, 1):
                remote(ids.at[my_id], ids.at[my_id], id_send.at[0], id_recv.at[0], around(0, d, j)).start()
        remote(ids.at[my_id], ids.at[my_id], id_send.at[0], id_recv.at[0], partner).start()
        expect(ids.at[pl.ds(0, 7)], id_send.at[0], id_recv.at[0], "id0")

    def ids_second():
        arrivals["id0"].wait_recv()
        view = ids.at[pl.ds(y * 8, 8)]
        for d in (1, -1, 2):
            remote(view, view, id_send.at[1], id_recv.at[1], around(1, d, core)).start()
        expect(ids.at[pl.ds(0, 24)], id_send.at[1], id_recv.at[1], "id1")

    def ids_done():
        arrivals["id1"].wait_recv()
        inv_v[...] = jnp.max(ids[...], axis=0)
        get = pltpu.make_async_copy(inv_v, inv_s, in_sem.at[5])
        get.start()
        for c in small:
            c.wait()
        for n in (0, 1):
            row = jnp.broadcast_to(vir_v[n : n + 1, :], (128, 128))
            vir_t[n * 128 : (n + 1) * 128, :] = row.T
        get.wait()
        get_lam.wait()
        give_lam.wait_recv()

    def multiply(k):
        arrivals[k, 2 if k in DIRECT else 3].wait_recv()

        def order(ab, carry):
            for ef in range(EF_T):
                tile = land[k][inv_s[0, ab * EF_T + ef]]
                rows = pl.ds(pl.multiple_of(ab * (2 * R), 2 * R), 2 * R)
                lhs[rows, ef * TILE : (ef + 1) * TILE] = tile.reshape(2 * R, TILE)
            return carry

        lax.fori_loop(0, AB_T, order, 0)

        def half(j, carry):
            for q in range(W2 // 256):
                cols = slice(q * 256, (q + 1) * 256)
                product = jnp.dot(lhs[...], lam_v[j, :, cols], preferred_element_type=jnp.float32)
                part[k][j, :, :, cols] = product.reshape(NZ, R, 256)
            return carry

        lax.fori_loop(0, 2, half, 0)
        far = stepz(z, 4)
        send, recv = h_send.at[k, 0], h_recv.at[k, 0]
        for n, d in enumerate((1, -1)):
            remote(part[k].at[n, far], hop0.at[k, n], send, recv, near_z(d)).start()
        expect(hop0.at[k], send, recv, (k, "h0"))
        give = remote(part[k].at[1 - core, z], swap.at[k], s_send.at[k], s_recv.at[k], partner)
        give.start()
        arrivals[k, "swap"] = give
        sent.append(give)

    def near_z(d):
        return dev(x, y, core, stepz(z, d))

    def hop_1(k):
        arrivals[k, "h0"].wait_recv()
        send, recv = h_send.at[k, 1], h_recv.at[k, 1]
        for n, d in enumerate((1, -1)):
            block = stepz(z, 3 * d)
            part[k][n, block] = part[k][n, block] + hop0[k, n]
            remote(part[k].at[:, block], hop1.at[k, n], send, recv, near_z(d)).start()
        expect(hop1.at[k], send, recv, (k, "h1"))

    def hop_2(k):
        arrivals[k, "h1"].wait_recv()
        send, recv = h_send.at[k, 2], h_recv.at[k, 2]
        for n, d in enumerate((1, -1)):
            block = stepz(z, 2 * d)
            part[k][:, block] = part[k][:, block] + hop1[k, n]
            remote(part[k].at[:, block], hop2.at[k, n], send, recv, near_z(d)).start()
        expect(hop2.at[k], send, recv, (k, "h2"))

    def hop_3(k):
        arrivals[k, "h2"].wait_recv()
        send, recv = h_send.at[k, 3], h_recv.at[k, 3]
        for n, d in enumerate((1, -1)):
            block = stepz(z, d)
            for j in (0, 1):
                part[k][j, block] = part[k][j, block] + hop2[k, n, j]
                remote(part[k].at[j, block], last.at[k, n, core], send, recv, updown[d][j]).start()
        expect(last.at[k], send, recv, (k, "h3"))

    def finish(k):
        arrivals[k, "swap"].wait_recv()
        arrivals[k, "h3"].wait_recv()
        for who, own in ((core, part[k][core, z]), (1 - core, swap[k])):
            rows = pl.ds(pl.multiple_of(who * 128 + k * R, R), R)
            ladder = own + last[k, 0, who] + last[k, 1, who]
            v = vir_t[rows, :]
            den = occ_v[...] - jnp.concatenate([v] * (W2 // 128), axis=1)
            out_ref[rows, :] = ((other_v[rows, :].astype(jnp.float32) + ladder) / den).astype(jnp.bfloat16)

    stage_1a(ORDER[0])
    ids_first()
    give_lam = remote(lam_ref, lam_v.at[core], lam_send, lam_recv, partner)
    give_lam.start()
    sent.append(give_lam)

    run = (stage_1a, stage_1b, stage_2a, stage_2b, multiply, hop_1, hop_2, hop_3, finish)
    first_2a = next(n for n, item in enumerate(ORDER) if item // 10 == S_2A)
    first_mm = next(n for n, item in enumerate(ORDER) if item // 10 == S_MM)
    for n, item in enumerate(ORDER):
        if n == first_2a:
            ids_second()
        if n == first_mm:
            ids_done()
        if n > 0:
            run[item // 10](item % 10)

    for c in sent:
        c.wait_send()


def body(w_tiles, task_ab, task_ef, lam_pairs, other_terms, vir_pair, occ_pair):
    w = w_tiles.reshape(2, 2, NK, R, TILE)
    anyspace = pl.BlockSpec(memory_space=pl.ANY)
    smem = pl.BlockSpec(memory_space=pltpu.SMEM)
    f32, bf16 = jnp.float32, jnp.bfloat16
    dma = pltpu.SemaphoreType.DMA
    scratch = [pltpu.VMEM((32, 2, R, TILE), bf16) for _ in range(NK)]
    scratch += [pltpu.VMEM((2, NZ, R, W2), f32) for _ in range(NK)]
    scratch += [
        pltpu.VMEM((2, 2, NK, R, TILE), bf16),
        pltpu.VMEM((2, EF_T * TILE, W2), bf16),
        pltpu.VMEM((AB_T * 2 * R, EF_T * TILE), bf16),
        pltpu.VMEM((NK, 2, R, W2), f32),
        pltpu.VMEM((NK, 2, 2, R, W2), f32),
        pltpu.VMEM((NK, 2, 2, R, W2), f32),
        pltpu.VMEM((NK, 2, 2, R, W2), f32),
        pltpu.VMEM((NK, R, W2), f32),
        pltpu.VMEM((256, W2), bf16),
        pltpu.VMEM((2, 128), f32),
        pltpu.VMEM((1, W2), f32),
        pltpu.VMEM((256, 128), f32),
        pltpu.VMEM((32, 1, 128), jnp.int32),
        pltpu.VMEM((1, 128), jnp.int32),
        pltpu.SMEM((1, 128), jnp.int32),
        dma((6,)),
        dma, dma,
        dma((2,)), dma((2,)),
        dma((NK, 4)), dma((NK, 4)),
        dma((NK, 4)), dma((NK, 4)),
        dma((NK,)), dma((NK,)),
    ]
    return pl.pallas_call(
        kernel,
        out_shape=jax.ShapeDtypeStruct((256, W2), bf16),
        in_specs=[smem, smem] + [anyspace] * 5,
        out_specs=pl.BlockSpec(memory_space=pltpu.VMEM),
        scratch_shapes=scratch,
        compiler_params=pltpu.CompilerParams(
            collective_id=0, has_side_effects=True, vmem_limit_bytes=VMEM
        ),
        cost_estimate=pl.CostEstimate(
            flops=2 * 2048 * 4096 * 512, bytes_accessed=6 * 1024 * 1024, transcendentals=0
        ),
    )(task_ab, task_ef, w, lam_pairs, other_terms, vir_pair.reshape(2, 128), occ_pair.reshape(1, W2))


def solution(mesh):
    placed = (
        P(("col", "row"), None, None),
        P(("col", "row")),
        P(("col", "row")),
        P("row", "col"),
        P("row", "col"),
        P("row"),
        P("col"),
    )
    return jax.shard_map(
        body, mesh=mesh, in_specs=placed, out_specs=P("row", "col"), check_vma=False
    )
```

```python
import jax
import jax.numpy as jnp
from jax import lax
from jax.experimental import pallas as pl
from jax.experimental.pallas import tpu as pltpu
from jax.sharding import PartitionSpec as P

TILE = 512
AB_T = 4
EF_T = 8
NX = NY = 4
NZ = 8
NK = 8
R = 16
W2 = 512
VMEM = 63 * 1024 * 1024

S_1A, S_1B, S_2A, S_2B, S_MM, S_H1, S_H2, S_H3, S_FIN = range(9)


ORDER = (
     2,  4,  1,  5,  3, 12,  0, 14,  6, 11,  7, 15, 22, 21, 17, 24,
    16, 13, 31, 10, 32, 23, 34, 25, 41, 42, 33, 51, 20, 52, 44, 35,
    61, 26, 43, 62, 30, 54, 27, 71, 45, 53, 64, 36, 72, 40, 55, 63,
    37, 74, 46, 50, 65, 47, 56, 84, 60, 57, 66, 75, 67, 73, 81, 82,
    70, 76, 77, 80, 85, 83, 86, 87,
)
DIRECT = ()


def split(v):
    high = v.astype(jnp.bfloat16)
    wide = high.astype(jnp.float32)
    most = jnp.max(jnp.abs(wide), axis=0, keepdims=True)
    scale = jnp.where(most > 1e-33, 32512.0 / most, 0.0)
    u = ((v - wide) * scale + 128.5).astype(jnp.int32)
    low = u[:, 384:]
    for part, bits in ((u[:, :128], 24), (u[:, 128:256], 16), (u[:, 256:384], 8)):
        low = low | lax.shift_left(part, jnp.full(part.shape, bits, jnp.int32))
    return high, low


def join(high, low):
    wide = high.astype(jnp.float32)
    most = jnp.max(jnp.abs(wide), axis=0, keepdims=True)
    parts = [
        lax.shift_right_logical(low, jnp.full(low.shape, bits, jnp.int32)) & 255 for bits in (24, 16, 8)
    ] + [low & 255]
    u = jnp.concatenate(parts, axis=1)
    return wide + (u - 128).astype(jnp.float32) * (most * (1.0 / 32512.0))


def kernel(ab_ref, ef_ref, w_ref, lam_ref, other_ref, vir_ref, occ_ref, out_ref, *scratch):
    land = scratch[:NK]
    part = scratch[NK : 2 * NK]
    (
        w_v, lam_v, lhs, hop0, hop1, hop2, last, low0, low1, low2, lowl, out0, outs, lout0, louts, swap, other_v, vir_v, occ_v, vir_t,
        ids, inv_v, inv_s,
        in_sem, lam_send, lam_recv, id_send, id_recv, g_send, g_recv,
        h_send, h_recv, s_send, s_recv,
    ) = scratch[2 * NK :]

    col = lax.axis_index("col")
    z = lax.axis_index("row")
    core = lax.rem(col, 2)
    y = lax.rem(col // 2, NY)
    x = col // (2 * NY)

    def dev(xx, yy, cc, zz):
        return ((xx * NY + yy) * 2 + cc, zz)

    def step4(v, d):
        return lax.rem(v + (4 + d), 4)

    def stepz(v, d):
        return lax.rem(v + (NZ + d), NZ)

    def remote(src, dst, send, recv, device):
        return pltpu.make_async_remote_copy(
            src_ref=src, dst_ref=dst, send_sem=send, recv_sem=recv,
            device_id=device, device_id_type=pl.DeviceIdType.MESH,
        )

    partner = dev(x, y, 1 - core, z)
    prime = (x, y)
    second = (y, x)
    near = {
        (axis, d, j): dev(step4(x, d), y, j, z) if axis == 0 else dev(x, step4(y, d), j, z)
        for axis in (0, 1) for d in (1, -1, 2) for j in (0, 1)
    }

    def around(axis, d, j):
        if axis == 0:
            return dev(step4(x, d), y, j, z)
        return dev(x, step4(y, d), j, z)

    updown = {d: [dev(x, y, j, stepz(z, d)) for j in (0, 1)] for d in (1, -1)}

    get_w = pltpu.make_async_copy(w_ref, w_v, in_sem.at[0])
    get_w.start()
    get_lam = pltpu.make_async_copy(lam_ref, lam_v.at[core], in_sem.at[1])
    get_lam.start()
    small = [
        pltpu.make_async_copy(vir_ref, vir_v, in_sem.at[2]),
        pltpu.make_async_copy(occ_ref, occ_v, in_sem.at[3]),
        pltpu.make_async_copy(other_ref, other_v, in_sem.at[4]),
    ]
    for c in small:
        c.start()

    barrier = pltpu.get_barrier_semaphore()
    greeted = [partner] + list(near.values()) + updown[1] + updown[-1]
    for who in greeted:
        pl.semaphore_signal(barrier, inc=1, device_id=who, device_id_type=pl.DeviceIdType.MESH)

    my_slot = core * 16 + jnp.where(core == 0, y * 4 + x, x * 4 + y)
    my_id = (y * 4 + x) * 2 + core
    code = ab_ref[0] * EF_T + ef_ref[0]
    lane = lax.broadcasted_iota(jnp.int32, (1, 128), 1)
    ids[my_id] = jnp.where(lane == code, my_slot, 0)
    get_w.wait()
    for k in range(NK):
        land[k][my_slot] = w_v[:, core, k]

    pl.semaphore_wait(barrier, len(greeted))

    sent = []

    def mine_along(d, j):
        xx = jnp.where(core == 0, step4(x, d), x)
        yy = jnp.where(core == 0, y, step4(y, d))
        return dev(xx, yy, j, z)

    def stage_1a(k):
        send, recv = g_send.at[k, 0], g_recv.at[k, 0]
        hops = (1, -1, 2) if k in DIRECT else (1, -1)
        for d in hops:
            for j in (0, 1):
                remote(w_v.at[:, j, k], land[k].at[my_slot], send, recv, mine_along(d, j)).start()
        remote(w_v.at[:, 1 - core, k], land[k].at[my_slot], send, recv, partner).start()
        expect(land[k].at[pl.ds(0, 2 * len(hops) + 1)], send, recv, (k, 0))

    arrivals = {}

    def expect(view, send, recv, key):
        both = remote(view, view, send, recv, partner)
        arrivals[key] = both
        sent.append(both)

    def slot(g, s, p):
        return g * 16 + s * 4 + p

    def stage_1b(k):
        arrivals[k, 0].wait_recv()
        send, recv = g_send.at[k, 1], g_recv.at[k, 1]
        for g in (0, 1):
            for n, d in enumerate((1, -1)):
                view = land[k].at[slot(g, second[g], step4(prime[g], -d)), n]
                remote(view, view, send, recv, around(g, d, core)).start()
        expect(land[k].at[pl.ds(0, 2)], send, recv, (k, 1))

    def stage_2a(k):
        arrivals[k, 0 if k in DIRECT else 1].wait_recv()
        send, recv = g_send.at[k, 2], g_recv.at[k, 2]
        hops = (1, -1, 2) if k in DIRECT else (1, -1)
        for g in (0, 1):
            view = land[k].at[pl.ds(slot(g, second[g], 0), 4)]
            for d in hops:
                remote(view, view, send, recv, around(1 - g, d, core)).start()
        expect(land[k].at[pl.ds(0, 8 * len(hops))], send, recv, (k, 2))

    def stage_2b(k):
        arrivals[k, 2].wait_recv()
        send, recv = g_send.at[k, 3], g_recv.at[k, 3]
        for g in (0, 1):
            for n, d in enumerate((1, -1)):
                view = land[k].at[pl.ds(slot(g, step4(second[g], -d), 2 * n), 2)]
                remote(view, view, send, recv, around(1 - g, d, core)).start()
        expect(land[k].at[pl.ds(0, 8)], send, recv, (k, 3))

    def ids_first():
        for d in (1, -1, 2):
            for j in (0, 1):
                remote(ids.at[my_id], ids.at[my_id], id_send.at[0], id_recv.at[0], around(0, d, j)).start()
        remote(ids.at[my_id], ids.at[my_id], id_send.at[0], id_recv.at[0], partner).start()
        expect(ids.at[pl.ds(0, 7)], id_send.at[0], id_recv.at[0], "id0")

    def ids_second():
        arrivals["id0"].wait_recv()
        view = ids.at[pl.ds(y * 8, 8)]
        for d in (1, -1, 2):
            remote(view, view, id_send.at[1], id_recv.at[1], around(1, d, core)).start()
        expect(ids.at[pl.ds(0, 24)], id_send.at[1], id_recv.at[1], "id1")

    def ids_done():
        arrivals["id1"].wait_recv()
        inv_v[...] = jnp.max(ids[...], axis=0)
        get = pltpu.make_async_copy(inv_v, inv_s, in_sem.at[5])
        get.start()
        for c in small:
            c.wait()
        for n in (0, 1):
            row = jnp.broadcast_to(vir_v[n : n + 1, :], (128, 128))
            vir_t[n * 128 : (n + 1) * 128, :] = row.T
        get.wait()
        get_lam.wait()
        give_lam.wait_recv()

    def multiply(k):
        arrivals[k, 2 if k in DIRECT else 3].wait_recv()

        def order(ab, carry):
            for ef in range(EF_T):
                tile = land[k][inv_s[0, ab * EF_T + ef]]
                rows = pl.ds(pl.multiple_of(ab * (2 * R), 2 * R), 2 * R)
                lhs[rows, ef * TILE : (ef + 1) * TILE] = tile.reshape(2 * R, TILE)
            return carry

        lax.fori_loop(0, AB_T, order, 0)

        def half(j, carry):
            for q in range(W2 // 256):
                cols = slice(q * 256, (q + 1) * 256)
                product = jnp.dot(lhs[...], lam_v[j, :, cols], preferred_element_type=jnp.float32)
                part[k][j, :, :, cols] = product.reshape(NZ, R, 256)
            return carry

        lax.fori_loop(0, 2, half, 0)
        far = stepz(z, 4)
        for n, d in enumerate((1, -1)):
            out0[k, n], lout0[k, n] = split(part[k][n, far])
            ship(k, 0, out0.at[k, n], lout0.at[k, n], hop0.at[k, n], low0.at[k, n], near_z(d))
        expect_both(k, 0, hop0.at[k], low0.at[k])
        give = remote(part[k].at[1 - core, z], swap.at[k], s_send.at[k], s_recv.at[k], partner)
        give.start()
        arrivals[k, "swap"] = give
        sent.append(give)

    def near_z(d):
        return dev(x, y, core, stepz(z, d))

    def ship(k, stage, high, low, high_to, low_to, who):
        remote(high, high_to, h_send.at[k, stage, 0], h_recv.at[k, stage, 0], who).start()
        remote(low, low_to, h_send.at[k, stage, 1], h_recv.at[k, stage, 1], who).start()

    def expect_both(k, stage, high, low):
        expect(high, h_send.at[k, stage, 0], h_recv.at[k, stage, 0], (k, "high", stage))
        expect(low, h_send.at[k, stage, 1], h_recv.at[k, stage, 1], (k, "low", stage))

    def arrived(k, stage):
        arrivals[k, "high", stage].wait_recv()
        arrivals[k, "low", stage].wait_recv()

    def hop_1(k):
        arrived(k, 0)
        for n, d in enumerate((1, -1)):
            block = stepz(z, 3 * d)
            for j in (0, 1):
                v = part[k][j, block]
                if j == n:
                    v = v + join(hop0[k, n], low0[k, n])
                outs[k, 0, n, j], louts[k, 0, n, j] = split(v)
            ship(k, 1, outs.at[k, 0, n], louts.at[k, 0, n], hop1.at[k, n], low1.at[k, n], near_z(d))
        expect_both(k, 1, hop1.at[k], low1.at[k])

    def hop_2(k):
        arrived(k, 1)
        for n, d in enumerate((1, -1)):
            block = stepz(z, 2 * d)
            for j in (0, 1):
                v = part[k][j, block] + join(hop1[k, n, j], low1[k, n, j])
                outs[k, 1, n, j], louts[k, 1, n, j] = split(v)
            ship(k, 2, outs.at[k, 1, n], louts.at[k, 1, n], hop2.at[k, n], low2.at[k, n], near_z(d))
        expect_both(k, 2, hop2.at[k], low2.at[k])

    def hop_3(k):
        arrived(k, 2)
        for n, d in enumerate((1, -1)):
            block = stepz(z, d)
            for j in (0, 1):
                v = part[k][j, block] + join(hop2[k, n, j], low2[k, n, j])
                outs[k, 2, n, j], louts[k, 2, n, j] = split(v)
                ship(
                    k, 3, outs.at[k, 2, n, j], louts.at[k, 2, n, j],
                    last.at[k, n, core], lowl.at[k, n, core], updown[d][j],
                )
        expect_both(k, 3, last.at[k], lowl.at[k])

    def finish(k):
        arrivals[k, "swap"].wait_recv()
        arrived(k, 3)
        for who, own in ((core, part[k][core, z]), (1 - core, swap[k])):
            rows = pl.ds(pl.multiple_of(who * 128 + k * R, R), R)
            ladder = own + join(last[k, 0, who], lowl[k, 0, who]) + join(last[k, 1, who], lowl[k, 1, who])
            v = vir_t[rows, :]
            den = occ_v[...] - jnp.concatenate([v] * (W2 // 128), axis=1)
            out_ref[rows, :] = ((other_v[rows, :].astype(jnp.float32) + ladder) / den).astype(jnp.bfloat16)

    stage_1a(ORDER[0])
    ids_first()
    give_lam = remote(lam_ref, lam_v.at[core], lam_send, lam_recv, partner)
    give_lam.start()
    sent.append(give_lam)

    run = (stage_1a, stage_1b, stage_2a, stage_2b, multiply, hop_1, hop_2, hop_3, finish)
    first_2a = next(n for n, item in enumerate(ORDER) if item // 10 == S_2A)
    first_mm = next(n for n, item in enumerate(ORDER) if item // 10 == S_MM)
    for n, item in enumerate(ORDER):
        if n == first_2a:
            ids_second()
        if n == first_mm:
            ids_done()
        if n > 0:
            run[item // 10](item % 10)

    for c in sent:
        c.wait_send()


def body(w_tiles, task_ab, task_ef, lam_pairs, other_terms, vir_pair, occ_pair):
    w = w_tiles.reshape(2, 2, NK, R, TILE)
    anyspace = pl.BlockSpec(memory_space=pl.ANY)
    smem = pl.BlockSpec(memory_space=pltpu.SMEM)
    f32, bf16 = jnp.float32, jnp.bfloat16
    dma = pltpu.SemaphoreType.DMA
    scratch = [pltpu.VMEM((32, 2, R, TILE), bf16) for _ in range(NK)]
    scratch += [pltpu.VMEM((2, NZ, R, W2), f32) for _ in range(NK)]
    scratch += [
        pltpu.VMEM((2, 2, NK, R, TILE), bf16),
        pltpu.VMEM((2, EF_T * TILE, W2), bf16),
        pltpu.VMEM((AB_T * 2 * R, EF_T * TILE), bf16),
        pltpu.VMEM((NK, 2, R, W2), bf16),
        pltpu.VMEM((NK, 2, 2, R, W2), bf16),
        pltpu.VMEM((NK, 2, 2, R, W2), bf16),
        pltpu.VMEM((NK, 2, 2, R, W2), bf16),
        pltpu.VMEM((NK, 2, R, 128), jnp.int32),
        pltpu.VMEM((NK, 2, 2, R, 128), jnp.int32),
        pltpu.VMEM((NK, 2, 2, R, 128), jnp.int32),
        pltpu.VMEM((NK, 2, 2, R, 128), jnp.int32),
        pltpu.VMEM((NK, 2, R, W2), bf16),
        pltpu.VMEM((NK, 3, 2, 2, R, W2), bf16),
        pltpu.VMEM((NK, 2, R, 128), jnp.int32),
        pltpu.VMEM((NK, 3, 2, 2, R, 128), jnp.int32),
        pltpu.VMEM((NK, R, W2), f32),
        pltpu.VMEM((256, W2), bf16),
        pltpu.VMEM((2, 128), f32),
        pltpu.VMEM((1, W2), f32),
        pltpu.VMEM((256, 128), f32),
        pltpu.VMEM((32, 1, 128), jnp.int32),
        pltpu.VMEM((1, 128), jnp.int32),
        pltpu.SMEM((1, 128), jnp.int32),
        dma((6,)),
        dma, dma,
        dma((2,)), dma((2,)),
        dma((NK, 4)), dma((NK, 4)),
        dma((NK, 4, 2)), dma((NK, 4, 2)),
        dma((NK,)), dma((NK,)),
    ]
    return pl.pallas_call(
        kernel,
        out_shape=jax.ShapeDtypeStruct((256, W2), bf16),
        in_specs=[smem, smem] + [anyspace] * 5,
        out_specs=pl.BlockSpec(memory_space=pltpu.VMEM),
        scratch_shapes=scratch,
        compiler_params=pltpu.CompilerParams(
            collective_id=0, has_side_effects=True, vmem_limit_bytes=VMEM
        ),
        cost_estimate=pl.CostEstimate(
            flops=2 * 2048 * 4096 * 512, bytes_accessed=6 * 1024 * 1024, transcendentals=0
        ),
    )(task_ab, task_ef, w, lam_pairs, other_terms, vir_pair.reshape(2, 128), occ_pair.reshape(1, W2))


def solution(mesh):
    placed = (
        P(("col", "row"), None, None),
        P(("col", "row")),
        P(("col", "row")),
        P("row", "col"),
        P("row", "col"),
        P("row"),
        P("col"),
    )
    return jax.shard_map(
        body, mesh=mesh, in_specs=placed, out_specs=P("row", "col"), check_vma=False
    )
```

```python
import jax
import jax.numpy as jnp
from jax import lax
from jax.experimental import pallas as pl
from jax.experimental.pallas import tpu as pltpu
from jax.sharding import PartitionSpec as P

TILE = 512
AB_T = 4
EF_T = 8
NX = NY = 4
NZ = 8
NK = 8
R = 16
W2 = 512
VMEM = 54784 * 1024

S_1A, S_1B, S_2A, S_2B, S_MM, S_H1, S_H2, S_H3, S_FIN = range(9)


ORDER = (
     2,  4,  1,  5,  3, 12,  0, 14,  6, 11,  7, 15, 22, 21, 17, 24,
    16, 13, 31, 10, 32, 23, 34, 25, 41, 42, 33, 51, 20, 52, 44, 35,
    61, 26, 43, 62, 30, 54, 27, 71, 45, 53, 64, 36, 72, 40, 55, 63,
    37, 74, 46, 50, 65, 47, 56, 84, 60, 57, 66, 75, 67, 73, 81, 82,
    70, 76, 77, 80, 85, 83, 86, 87,
)
DIRECT = ()


def split(v):
    high = v.astype(jnp.bfloat16)
    wide = high.astype(jnp.float32)
    most = jnp.max(jnp.abs(wide), axis=0, keepdims=True)
    scale = jnp.where(most > 1e-33, 32512.0 / most, 0.0)
    u = ((v - wide) * scale + 128.5).astype(jnp.int32)
    low = u[:, 384:]
    for part, bits in ((u[:, :128], 24), (u[:, 128:256], 16), (u[:, 256:384], 8)):
        low = low | lax.shift_left(part, jnp.full(part.shape, bits, jnp.int32))
    return high, low


def join(high, low):
    wide = high.astype(jnp.float32)
    most = jnp.max(jnp.abs(wide), axis=0, keepdims=True)
    parts = [
        lax.shift_right_logical(low, jnp.full(low.shape, bits, jnp.int32)) & 255 for bits in (24, 16, 8)
    ] + [low & 255]
    u = jnp.concatenate(parts, axis=1)
    return wide + (u - 128).astype(jnp.float32) * (most * (1.0 / 32512.0))


def kernel(ab_ref, ef_ref, w_ref, lam_ref, other_ref, vir_ref, occ_ref, out_ref, *scratch):
    land = scratch[:NK]
    part = scratch[NK : 2 * NK]
    (
        w_v, lam_v, lhs, hop0, hop1, hop2, last, low0, low1, low2, lowl, out0, outs, lout0, louts, swap, other_v, vir_v, occ_v, vir_t,
        ids, inv_v, inv_s,
        in_sem, lam_send, lam_recv, id_send, id_recv, c_send, g_recv, h_recv, s_recv,
    ) = scratch[2 * NK :]

    col = lax.axis_index("col")
    z = lax.axis_index("row")
    core = lax.rem(col, 2)
    y = lax.rem(col // 2, NY)
    x = col // (2 * NY)

    def dev(xx, yy, cc, zz):
        return ((xx * NY + yy) * 2 + cc, zz)

    def step4(v, d):
        return lax.rem(v + (4 + d), 4)

    def stepz(v, d):
        return lax.rem(v + (NZ + d), NZ)

    def remote(src, dst, send, recv, device):
        return pltpu.make_async_remote_copy(
            src_ref=src, dst_ref=dst, send_sem=send, recv_sem=recv,
            device_id=device, device_id_type=pl.DeviceIdType.MESH,
        )

    partner = dev(x, y, 1 - core, z)
    prime = (x, y)
    second = (y, x)
    near = {
        (axis, d, j): dev(step4(x, d), y, j, z) if axis == 0 else dev(x, step4(y, d), j, z)
        for axis in (0, 1) for d in (1, -1, 2) for j in (0, 1)
    }

    def around(axis, d, j):
        if axis == 0:
            return dev(step4(x, d), y, j, z)
        return dev(x, step4(y, d), j, z)

    updown = {d: [dev(x, y, j, stepz(z, d)) for j in (0, 1)] for d in (1, -1)}

    get_w = pltpu.make_async_copy(w_ref, w_v, in_sem.at[0])
    get_w.start()
    get_lam = pltpu.make_async_copy(lam_ref, lam_v.at[core], in_sem.at[1])
    get_lam.start()
    small = [
        pltpu.make_async_copy(vir_ref, vir_v, in_sem.at[2]),
        pltpu.make_async_copy(occ_ref, occ_v, in_sem.at[3]),
        pltpu.make_async_copy(other_ref, other_v, in_sem.at[4]),
    ]
    for c in small:
        c.start()

    barrier = pltpu.get_barrier_semaphore()
    greeted = [partner] + list(near.values()) + updown[1] + updown[-1]
    for who in greeted:
        pl.semaphore_signal(barrier, inc=1, device_id=who, device_id_type=pl.DeviceIdType.MESH)

    my_slot = core * 16 + jnp.where(core == 0, y * 4 + x, x * 4 + y)
    my_id = (y * 4 + x) * 2 + core
    code = ab_ref[0] * EF_T + ef_ref[0]
    lane = lax.broadcasted_iota(jnp.int32, (1, 128), 1)
    ids[my_id] = jnp.where(lane == code, my_slot, 0)
    get_w.wait()
    for k in range(NK):
        land[k][my_slot] = w_v[:, core, k]

    pl.semaphore_wait(barrier, len(greeted))

    def mine_along(d, j):
        xx = jnp.where(core == 0, step4(x, d), x)
        yy = jnp.where(core == 0, y, step4(y, d))
        return dev(xx, yy, j, z)

    def stage_1a(k):
        send, recv = c_send.at[k], g_recv.at[k, 0]
        hops = (1, -1, 2) if k in DIRECT else (1, -1)
        for d in hops:
            for j in (0, 1):
                remote(w_v.at[:, j, k], land[k].at[my_slot], send, recv, mine_along(d, j)).start()
        remote(w_v.at[:, 1 - core, k], land[k].at[my_slot], send, recv, partner).start()
        expect(land[k].at[pl.ds(0, 2 * len(hops) + 1)], send, recv, (k, 0))

    arrivals = {}

    def expect(view, send, recv, key):
        arrivals[key] = remote(view, view, send, recv, partner)

    def slot(g, s, p):
        return g * 16 + s * 4 + p

    def stage_1b(k):
        arrivals[k, 0].wait_recv()
        send, recv = c_send.at[k], g_recv.at[k, 1]
        for g in (0, 1):
            for n, d in enumerate((1, -1)):
                view = land[k].at[slot(g, second[g], step4(prime[g], -d)), n]
                remote(view, view, send, recv, around(g, d, core)).start()
        expect(land[k].at[pl.ds(0, 2)], send, recv, (k, 1))

    def stage_2a(k):
        arrivals[k, 0 if k in DIRECT else 1].wait_recv()
        send, recv = c_send.at[k], g_recv.at[k, 2]
        hops = (1, -1, 2) if k in DIRECT else (1, -1)
        for g in (0, 1):
            view = land[k].at[pl.ds(slot(g, second[g], 0), 4)]
            for d in hops:
                remote(view, view, send, recv, around(1 - g, d, core)).start()
        expect(land[k].at[pl.ds(0, 8 * len(hops))], send, recv, (k, 2))

    def stage_2b(k):
        arrivals[k, 2].wait_recv()
        send, recv = c_send.at[k], g_recv.at[k, 3]
        for g in (0, 1):
            for n, d in enumerate((1, -1)):
                view = land[k].at[pl.ds(slot(g, step4(second[g], -d), 2 * n), 2)]
                remote(view, view, send, recv, around(1 - g, d, core)).start()
        expect(land[k].at[pl.ds(0, 8)], send, recv, (k, 3))

    def ids_first():
        for d in (1, -1, 2):
            for j in (0, 1):
                remote(ids.at[my_id], ids.at[my_id], id_send.at[0], id_recv.at[0], around(0, d, j)).start()
        remote(ids.at[my_id], ids.at[my_id], id_send.at[0], id_recv.at[0], partner).start()
        expect(ids.at[pl.ds(0, 7)], id_send.at[0], id_recv.at[0], "id0")

    def ids_second():
        arrivals["id0"].wait_recv()
        view = ids.at[pl.ds(y * 8, 8)]
        for d in (1, -1, 2):
            remote(view, view, id_send.at[1], id_recv.at[1], around(1, d, core)).start()
        expect(ids.at[pl.ds(0, 24)], id_send.at[1], id_recv.at[1], "id1")

    def ids_done():
        arrivals["id1"].wait_recv()
        inv_v[...] = jnp.max(ids[...], axis=0)
        get = pltpu.make_async_copy(inv_v, inv_s, in_sem.at[5])
        get.start()
        for c in small:
            c.wait()
        for n in (0, 1):
            row = jnp.broadcast_to(vir_v[n : n + 1, :], (128, 128))
            vir_t[n * 128 : (n + 1) * 128, :] = row.T
        get.wait()
        get_lam.wait()
        give_lam.wait_recv()

    def multiply(k):
        arrivals[k, 2 if k in DIRECT else 3].wait_recv()

        def order(ab, carry):
            for ef in range(EF_T):
                tile = land[k][inv_s[0, ab * EF_T + ef]]
                rows = pl.ds(pl.multiple_of(ab * (2 * R), 2 * R), 2 * R)
                lhs[rows, ef * TILE : (ef + 1) * TILE] = tile.reshape(2 * R, TILE)
            return carry

        lax.fori_loop(0, AB_T, order, 0)

        def half(j, carry):
            for q in range(W2 // 256):
                cols = slice(q * 256, (q + 1) * 256)
                product = jnp.dot(lhs[...], lam_v[j, :, cols], preferred_element_type=jnp.float32)
                part[k][j, :, :, cols] = product.reshape(NZ, R, 256)
            return carry

        lax.fori_loop(0, 2, half, 0)
        far = stepz(z, 4)
        for n, d in enumerate((1, -1)):
            out0[k, n], lout0[k, n] = split(part[k][n, far])
            ship(k, 0, out0.at[k, n], lout0.at[k, n], hop0.at[k, n], low0.at[k, n], near_z(d))
        expect_hop(k, 0)
        give = remote(part[k].at[1 - core, z], swap.at[k], c_send.at[k], s_recv.at[k], partner)
        give.start()
        arrivals[k, "swap"] = give

    def near_z(d):
        return dev(x, y, core, stepz(z, d))

    def ship(k, stage, high, low, high_to, low_to, who):
        remote(high, high_to, c_send.at[k], h_recv.at[k, stage], who).start()
        remote(low, low_to, c_send.at[k], h_recv.at[k, stage], who).start()

    def expect_hop(k, stage):
        expect(lam_v.at[0, pl.ds(0, 48 if stage == 0 else 96)], c_send.at[k], h_recv.at[k, stage], (k, "hop", stage))

    def arrived(k, stage):
        arrivals[k, "hop", stage].wait_recv()

    def hop_1(k):
        arrived(k, 0)
        for n, d in enumerate((1, -1)):
            block = stepz(z, 3 * d)
            for j in (0, 1):
                v = part[k][j, block]
                if j == n:
                    v = v + join(hop0[k, n], low0[k, n])
                outs[k, 0, n, j], louts[k, 0, n, j] = split(v)
            ship(k, 1, outs.at[k, 0, n], louts.at[k, 0, n], hop1.at[k, n], low1.at[k, n], near_z(d))
        expect_hop(k, 1)

    def hop_2(k):
        arrived(k, 1)
        for n, d in enumerate((1, -1)):
            block = stepz(z, 2 * d)
            for j in (0, 1):
                v = part[k][j, block] + join(hop1[k, n, j], low1[k, n, j])
                outs[k, 1, n, j], louts[k, 1, n, j] = split(v)
            ship(k, 2, outs.at[k, 1, n], louts.at[k, 1, n], hop2.at[k, n], low2.at[k, n], near_z(d))
        expect_hop(k, 2)

    def hop_3(k):
        arrived(k, 2)
        for n, d in enumerate((1, -1)):
            block = stepz(z, d)
            for j in (0, 1):
                v = part[k][j, block] + join(hop2[k, n, j], low2[k, n, j])
                outs[k, 2, n, j], louts[k, 2, n, j] = split(v)
                ship(
                    k, 3, outs.at[k, 2, n, j], louts.at[k, 2, n, j],
                    last.at[k, n, core], lowl.at[k, n, core], updown[d][j],
                )
        expect_hop(k, 3)

    def finish(k):
        arrivals[k, "swap"].wait_recv()
        arrived(k, 3)
        for who, own in ((core, part[k][core, z]), (1 - core, swap[k])):
            rows = pl.ds(pl.multiple_of(who * 128 + k * R, R), R)
            ladder = own + join(last[k, 0, who], lowl[k, 0, who]) + join(last[k, 1, who], lowl[k, 1, who])
            v = vir_t[rows, :]
            den = occ_v[...] - jnp.concatenate([v] * (W2 // 128), axis=1)
            out_ref[rows, :] = ((other_v[rows, :].astype(jnp.float32) + ladder) / den).astype(jnp.bfloat16)

    stage_1a(ORDER[0])
    ids_first()
    give_lam = remote(lam_ref, lam_v.at[core], lam_send, lam_recv, partner)
    give_lam.start()

    run = (stage_1a, stage_1b, stage_2a, stage_2b, multiply, hop_1, hop_2, hop_3, finish)
    first_2a = next(n for n, item in enumerate(ORDER) if item // 10 == S_2A)
    first_mm = next(n for n, item in enumerate(ORDER) if item // 10 == S_MM)
    for n, item in enumerate(ORDER):
        if n == first_2a:
            ids_second()
        if n == first_mm:
            ids_done()
        if n > 0:
            run[item // 10](item % 10)

    for key in ("id0", "id1"):
        arrivals[key].wait_send()
    give_lam.wait_send()
    for k in range(NK):
        first = 7 * 32 if k in DIRECT else 5 * 32
        plane = first + (24 * 32 if k in DIRECT else 64 + 512 + 256)
        view = lam_v.at[0, pl.ds(0, plane + 48 + 3 * 96 + 32)]
        remote(view, view, c_send.at[k], s_recv.at[k], partner).wait_send()


def body(w_tiles, task_ab, task_ef, lam_pairs, other_terms, vir_pair, occ_pair):
    w = w_tiles.reshape(2, 2, NK, R, TILE)
    anyspace = pl.BlockSpec(memory_space=pl.ANY)
    smem = pl.BlockSpec(memory_space=pltpu.SMEM)
    f32, bf16 = jnp.float32, jnp.bfloat16
    dma = pltpu.SemaphoreType.DMA
    scratch = [pltpu.VMEM((32, 2, R, TILE), bf16) for _ in range(NK)]
    scratch += [pltpu.VMEM((2, NZ, R, W2), f32) for _ in range(NK)]
    scratch += [
        pltpu.VMEM((2, 2, NK, R, TILE), bf16),
        pltpu.VMEM((2, EF_T * TILE, W2), bf16),
        pltpu.VMEM((AB_T * 2 * R, EF_T * TILE), bf16),
        pltpu.VMEM((NK, 2, R, W2), bf16),
        pltpu.VMEM((NK, 2, 2, R, W2), bf16),
        pltpu.VMEM((NK, 2, 2, R, W2), bf16),
        pltpu.VMEM((NK, 2, 2, R, W2), bf16),
        pltpu.VMEM((NK, 2, R, 128), jnp.int32),
        pltpu.VMEM((NK, 2, 2, R, 128), jnp.int32),
        pltpu.VMEM((NK, 2, 2, R, 128), jnp.int32),
        pltpu.VMEM((NK, 2, 2, R, 128), jnp.int32),
        pltpu.VMEM((NK, 2, R, W2), bf16),
        pltpu.VMEM((NK, 3, 2, 2, R, W2), bf16),
        pltpu.VMEM((NK, 2, R, 128), jnp.int32),
        pltpu.VMEM((NK, 3, 2, 2, R, 128), jnp.int32),
        pltpu.VMEM((NK, R, W2), f32),
        pltpu.VMEM((256, W2), bf16),
        pltpu.VMEM((2, 128), f32),
        pltpu.VMEM((1, W2), f32),
        pltpu.VMEM((256, 128), f32),
        pltpu.VMEM((32, 1, 128), jnp.int32),
        pltpu.VMEM((1, 128), jnp.int32),
        pltpu.SMEM((1, 128), jnp.int32),
        dma((6,)),
        dma, dma,
        dma((2,)), dma((2,)),
        dma((NK,)), dma((NK, 4)),
        dma((NK, 4)), dma((NK,)),
    ]
    return pl.pallas_call(
        kernel,
        out_shape=jax.ShapeDtypeStruct((256, W2), bf16),
        in_specs=[smem, smem] + [anyspace] * 5,
        out_specs=pl.BlockSpec(memory_space=pltpu.VMEM),
        scratch_shapes=scratch,
        compiler_params=pltpu.CompilerParams(
            collective_id=0, has_side_effects=True, vmem_limit_bytes=VMEM
        ),
        cost_estimate=pl.CostEstimate(
            flops=2 * 2048 * 4096 * 512, bytes_accessed=6 * 1024 * 1024, transcendentals=0
        ),
    )(task_ab, task_ef, w, lam_pairs, other_terms, vir_pair.reshape(2, 128), occ_pair.reshape(1, W2))


def solution(mesh):
    placed = (
        P(("col", "row"), None, None),
        P(("col", "row")),
        P(("col", "row")),
        P("row", "col"),
        P("row", "col"),
        P("row"),
        P("col"),
    )
    return jax.shard_map(
        body, mesh=mesh, in_specs=placed, out_specs=P("row", "col"), check_vma=False
    )
```

```python
import jax
import jax.numpy as jnp
from jax import lax
from jax.experimental import pallas as pl
from jax.experimental.pallas import tpu as pltpu
from jax.sharding import PartitionSpec as P

TILE = 512
AB_T = 4
EF_T = 8
NX = NY = 4
NZ = 8
NK = 8
R = 16
W2 = 512
VMEM = 54784 * 1024

S_1A, S_1B, S_2A, S_2B, S_MM, S_H1, S_H2, S_H3, S_FIN = range(9)


ORDER = (
     2,  4,  1,  5,  3, 12,  0, 14,  6, 11,  7, 15, 22, 21, 17, 24,
    16, 13, 31, 10, 32, 23, 34, 25, 41, 42, 33, 51, 20, 52, 44, 35,
    61, 26, 43, 62, 30, 54, 27, 71, 45, 53, 64, 36, 72, 40, 55, 63,
    37, 74, 46, 50, 65, 47, 56, 84, 60, 57, 66, 75, 67, 73, 81, 82,
    70, 76, 77, 80, 85, 83, 86, 87,
)
DIRECT = ()


def split(v):
    high = v.astype(jnp.bfloat16)
    wide = high.astype(jnp.float32)
    most = jnp.max(jnp.abs(wide), axis=0, keepdims=True)
    scale = jnp.where(most > 1e-33, 32512.0 / most, 0.0)
    u = ((v - wide) * scale + 128.5).astype(jnp.int32)
    low = u[:, 384:]
    for part, bits in ((u[:, :128], 24), (u[:, 128:256], 16), (u[:, 256:384], 8)):
        low = low | lax.shift_left(part, jnp.full(part.shape, bits, jnp.int32))
    return high, low


def join(high, low):
    wide = high.astype(jnp.float32)
    most = jnp.max(jnp.abs(wide), axis=0, keepdims=True)
    parts = [
        lax.shift_right_logical(low, jnp.full(low.shape, bits, jnp.int32)) & 255 for bits in (24, 16, 8)
    ] + [low & 255]
    u = jnp.concatenate(parts, axis=1)
    return wide + (u - 128).astype(jnp.float32) * (most * (1.0 / 32512.0))


def kernel(ab_ref, ef_ref, w_ref, lam_ref, other_ref, vir_ref, occ_ref, out_ref, *scratch):
    land = scratch[:NK]
    part = scratch[NK : 2 * NK]
    (
        w_v, lam_v, lhs, hop0, hop1, hop2, last, low0, low1, low2, lowl, out0, outs, lout0, louts, swap, other_v, vir_v, occ_v, vir_t,
        ids, inv_v, inv_s,
        in_sem, lam_send, lam_recv, id_send, id_recv, c_send, g_recv, h_recv, s_recv,
    ) = scratch[2 * NK :]

    col = lax.axis_index("col")
    z = lax.axis_index("row")
    core = lax.rem(col, 2)
    y = lax.rem(col // 2, NY)
    x = col // (2 * NY)

    def dev(xx, yy, cc, zz):
        return ((xx * NY + yy) * 2 + cc, zz)

    def step4(v, d):
        return lax.rem(v + (4 + d), 4)

    def stepz(v, d):
        return lax.rem(v + (NZ + d), NZ)

    def remote(src, dst, send, recv, device):
        return pltpu.make_async_remote_copy(
            src_ref=src, dst_ref=dst, send_sem=send, recv_sem=recv,
            device_id=device, device_id_type=pl.DeviceIdType.MESH,
        )

    partner = dev(x, y, 1 - core, z)
    prime = (x, y)
    second = (y, x)
    near = {
        (axis, d, j): dev(step4(x, d), y, j, z) if axis == 0 else dev(x, step4(y, d), j, z)
        for axis in (0, 1) for d in (1, -1, 2) for j in (0, 1)
    }

    def around(axis, d, j):
        if axis == 0:
            return dev(step4(x, d), y, j, z)
        return dev(x, step4(y, d), j, z)

    updown = {d: [dev(x, y, j, stepz(z, d)) for j in (0, 1)] for d in (1, -1)}

    get_w = pltpu.make_async_copy(w_ref, w_v, in_sem.at[0])
    get_w.start()
    get_lam = pltpu.make_async_copy(lam_ref, lam_v.at[core], in_sem.at[1])
    get_lam.start()
    small = [
        pltpu.make_async_copy(vir_ref, vir_v, in_sem.at[2]),
        pltpu.make_async_copy(occ_ref, occ_v, in_sem.at[3]),
        pltpu.make_async_copy(other_ref, other_v, in_sem.at[4]),
    ]
    for c in small:
        c.start()

    barrier = pltpu.get_barrier_semaphore()
    greeted = [partner] + list(near.values()) + updown[1] + updown[-1]
    for who in greeted:
        pl.semaphore_signal(barrier, inc=1, device_id=who, device_id_type=pl.DeviceIdType.MESH)

    my_slot = core * 16 + jnp.where(core == 0, y * 4 + x, x * 4 + y)
    my_id = (y * 4 + x) * 2 + core
    code = ab_ref[0] * EF_T + ef_ref[0]
    lane = lax.broadcasted_iota(jnp.int32, (1, 128), 1)
    ids[my_id] = jnp.where(lane == code, my_slot, 0)
    get_w.wait()
    for k in range(NK):
        land[k][my_slot] = w_v[:, core, k]

    pl.semaphore_wait(barrier, len(greeted))

    def mine_along(d, j):
        xx = jnp.where(core == 0, step4(x, d), x)
        yy = jnp.where(core == 0, y, step4(y, d))
        return dev(xx, yy, j, z)

    def stage_1a(k):
        send, recv = c_send.at[k], g_recv.at[k, 0]
        hops = (1, -1, 2) if k in DIRECT else (1, -1)
        for d in hops:
            for j in (0, 1):
                remote(w_v.at[:, j, k], land[k].at[my_slot], send, recv, mine_along(d, j)).start()
        remote(w_v.at[:, 1 - core, k], land[k].at[my_slot], send, recv, partner).start()
        expect(land[k].at[pl.ds(0, 2 * len(hops) + 1)], send, recv, (k, 0))

    arrivals = {}

    def expect(view, send, recv, key):
        arrivals[key] = remote(view, view, send, recv, partner)

    def slot(g, s, p):
        return g * 16 + s * 4 + p

    def stage_1b(k):
        arrivals[k, 0].wait_recv()
        send, recv = c_send.at[k], g_recv.at[k, 1]
        for g in (0, 1):
            for n, d in enumerate((1, -1)):
                view = land[k].at[slot(g, second[g], step4(prime[g], -d)), n]
                remote(view, view, send, recv, around(g, d, core)).start()
        expect(land[k].at[pl.ds(0, 2)], send, recv, (k, 1))

    def stage_2a(k):
        arrivals[k, 0 if k in DIRECT else 1].wait_recv()
        send, recv = c_send.at[k], g_recv.at[k, 2]
        hops = (1, -1, 2) if k in DIRECT else (1, -1)
        for g in (0, 1):
            view = land[k].at[pl.ds(slot(g, second[g], 0), 4)]
            for d in hops:
                remote(view, view, send, recv, around(1 - g, d, core)).start()
        expect(land[k].at[pl.ds(0, 8 * len(hops))], send, recv, (k, 2))

    def stage_2b(k):
        arrivals[k, 2].wait_recv()
        send, recv = c_send.at[k], g_recv.at[k, 3]
        for g in (0, 1):
            for n, d in enumerate((1, -1)):
                view = land[k].at[pl.ds(slot(g, step4(second[g], -d), 2 * n), 2)]
                remote(view, view, send, recv, around(1 - g, d, core)).start()
        expect(land[k].at[pl.ds(0, 8)], send, recv, (k, 3))

    def ids_first():
        for d in (1, -1, 2):
            for j in (0, 1):
                remote(ids.at[my_id], ids.at[my_id], id_send.at[0], id_recv.at[0], around(0, d, j)).start()
        remote(ids.at[my_id], ids.at[my_id], id_send.at[0], id_recv.at[0], partner).start()
        expect(ids.at[pl.ds(0, 7)], id_send.at[0], id_recv.at[0], "id0")

    def ids_second():
        arrivals["id0"].wait_recv()
        view = ids.at[pl.ds(y * 8, 8)]
        for d in (1, -1, 2):
            remote(view, view, id_send.at[1], id_recv.at[1], around(1, d, core)).start()
        expect(ids.at[pl.ds(0, 24)], id_send.at[1], id_recv.at[1], "id1")

    def ids_done():
        arrivals["id1"].wait_recv()
        inv_v[...] = jnp.max(ids[...], axis=0)
        get = pltpu.make_async_copy(inv_v, inv_s, in_sem.at[5])
        get.start()
        for c in small:
            c.wait()
        for n in (0, 1):
            row = jnp.broadcast_to(vir_v[n : n + 1, :], (128, 128))
            vir_t[n * 128 : (n + 1) * 128, :] = row.T
        get.wait()
        get_lam.wait()
        give_lam.wait_recv()

    def multiply(k):
        arrivals[k, 2 if k in DIRECT else 3].wait_recv()

        def order(ab, carry):
            for ef in range(EF_T):
                tile = land[k][inv_s[0, ab * EF_T + ef]]
                rows = pl.ds(pl.multiple_of(ab * (2 * R), 2 * R), 2 * R)
                lhs[rows, ef * TILE : (ef + 1) * TILE] = tile.reshape(2 * R, TILE)
            return carry

        lax.fori_loop(0, AB_T, order, 0)

        def half(j, carry):
            for q in range(W2 // 256):
                cols = slice(q * 256, (q + 1) * 256)
                product = jnp.dot(lhs[...], lam_v[j, :, cols], preferred_element_type=jnp.float32)
                part[k][j, :, :, cols] = product.reshape(NZ, R, 256)
            return carry

        lax.fori_loop(0, 2, half, 0)
        far = stepz(z, 4)
        for n, d in enumerate((1, -1)):
            out0[k, n], lout0[k, n] = split(part[k][n, far])
            ship(k, 0, out0.at[k, n], lout0.at[k, n], hop0.at[k, n], low0.at[k, n], near_z(d))
        expect_hop(k, 0)
        give = remote(part[k].at[1 - core, z], swap.at[k], c_send.at[k], s_recv.at[k], partner)
        give.start()
        arrivals[k, "swap"] = give

    def near_z(d):
        return dev(x, y, core, stepz(z, d))

    def ship(k, stage, high, low, high_to, low_to, who):
        remote(high, high_to, c_send.at[k], h_recv.at[k, stage], who).start()
        remote(low, low_to, c_send.at[k], h_recv.at[k, stage], who).start()

    def expect_hop(k, stage):
        expect(lam_v.at[0, pl.ds(0, 48 if stage == 0 else 96)], c_send.at[k], h_recv.at[k, stage], (k, "hop", stage))

    def arrived(k, stage):
        arrivals[k, "hop", stage].wait_recv()

    def hop_1(k):
        arrived(k, 0)
        for n, d in enumerate((1, -1)):
            block = stepz(z, 3 * d)
            for j in (0, 1):
                v = part[k][j, block]
                if j == n:
                    v = v + join(hop0[k, n], low0[k, n])
                outs[k, 0, n, j], louts[k, 0, n, j] = split(v)
            ship(k, 1, outs.at[k, 0, n], louts.at[k, 0, n], hop1.at[k, n], low1.at[k, n], near_z(d))
        expect_hop(k, 1)

    def hop_2(k):
        arrived(k, 1)
        for n, d in enumerate((1, -1)):
            block = stepz(z, 2 * d)
            for j in (0, 1):
                v = part[k][j, block] + join(hop1[k, n, j], low1[k, n, j])
                outs[k, 1, n, j], louts[k, 1, n, j] = split(v)
            ship(k, 2, outs.at[k, 1, n], louts.at[k, 1, n], hop2.at[k, n], low2.at[k, n], near_z(d))
        expect_hop(k, 2)

    def hop_3(k):
        arrived(k, 2)
        for n, d in enumerate((1, -1)):
            block = stepz(z, d)
            for j in (0, 1):
                v = part[k][j, block] + join(hop2[k, n, j], low2[k, n, j])
                outs[k, 2, n, j], louts[k, 2, n, j] = split(v)
                ship(
                    k, 3, outs.at[k, 2, n, j], louts.at[k, 2, n, j],
                    last.at[k, n, core], lowl.at[k, n, core], updown[d][j],
                )
        expect_hop(k, 3)

    def finish(k):
        arrivals[k, "swap"].wait_recv()
        arrived(k, 3)
        for who, own in ((core, part[k][core, z]), (1 - core, swap[k])):
            rows = pl.ds(pl.multiple_of(who * 128 + k * R, R), R)
            ladder = own + join(last[k, 0, who], lowl[k, 0, who]) + join(last[k, 1, who], lowl[k, 1, who])
            v = vir_t[rows, :]
            den = occ_v[...] - jnp.concatenate([v] * (W2 // 128), axis=1)
            out_ref[rows, :] = ((other_v[rows, :].astype(jnp.float32) + ladder) / den).astype(jnp.bfloat16)

    stage_1a(ORDER[0])
    ids_first()
    give_lam = remote(lam_ref, lam_v.at[core], lam_send, lam_recv, partner)

    run = (stage_1a, stage_1b, stage_2a, stage_2b, multiply, hop_1, hop_2, hop_3, finish)
    first_2a = next(n for n, item in enumerate(ORDER) if item // 10 == S_2A)
    first_mm = next(n for n, item in enumerate(ORDER) if item // 10 == S_MM)
    for n, item in enumerate(ORDER):
        if n == first_2a:
            ids_second()
            give_lam.start()
        if n == first_mm:
            ids_done()
        if n > 0:
            run[item // 10](item % 10)

    for key in ("id0", "id1"):
        arrivals[key].wait_send()
    give_lam.wait_send()
    for k in range(NK):
        first = 7 * 32 if k in DIRECT else 5 * 32
        plane = first + (24 * 32 if k in DIRECT else 64 + 512 + 256)
        view = lam_v.at[0, pl.ds(0, plane + 48 + 3 * 96 + 32)]
        remote(view, view, c_send.at[k], s_recv.at[k], partner).wait_send()


def body(w_tiles, task_ab, task_ef, lam_pairs, other_terms, vir_pair, occ_pair):
    w = w_tiles.reshape(2, 2, NK, R, TILE)
    anyspace = pl.BlockSpec(memory_space=pl.ANY)
    smem = pl.BlockSpec(memory_space=pltpu.SMEM)
    f32, bf16 = jnp.float32, jnp.bfloat16
    dma = pltpu.SemaphoreType.DMA
    scratch = [pltpu.VMEM((32, 2, R, TILE), bf16) for _ in range(NK)]
    scratch += [pltpu.VMEM((2, NZ, R, W2), f32) for _ in range(NK)]
    scratch += [
        pltpu.VMEM((2, 2, NK, R, TILE), bf16),
        pltpu.VMEM((2, EF_T * TILE, W2), bf16),
        pltpu.VMEM((AB_T * 2 * R, EF_T * TILE), bf16),
        pltpu.VMEM((NK, 2, R, W2), bf16),
        pltpu.VMEM((NK, 2, 2, R, W2), bf16),
        pltpu.VMEM((NK, 2, 2, R, W2), bf16),
        pltpu.VMEM((NK, 2, 2, R, W2), bf16),
        pltpu.VMEM((NK, 2, R, 128), jnp.int32),
        pltpu.VMEM((NK, 2, 2, R, 128), jnp.int32),
        pltpu.VMEM((NK, 2, 2, R, 128), jnp.int32),
        pltpu.VMEM((NK, 2, 2, R, 128), jnp.int32),
        pltpu.VMEM((NK, 2, R, W2), bf16),
        pltpu.VMEM((NK, 3, 2, 2, R, W2), bf16),
        pltpu.VMEM((NK, 2, R, 128), jnp.int32),
        pltpu.VMEM((NK, 3, 2, 2, R, 128), jnp.int32),
        pltpu.VMEM((NK, R, W2), f32),
        pltpu.VMEM((256, W2), bf16),
        pltpu.VMEM((2, 128), f32),
        pltpu.VMEM((1, W2), f32),
        pltpu.VMEM((256, 128), f32),
        pltpu.VMEM((32, 1, 128), jnp.int32),
        pltpu.VMEM((1, 128), jnp.int32),
        pltpu.SMEM((1, 128), jnp.int32),
        dma((6,)),
        dma, dma,
        dma((2,)), dma((2,)),
        dma((NK,)), dma((NK, 4)),
        dma((NK, 4)), dma((NK,)),
    ]
    return pl.pallas_call(
        kernel,
        out_shape=jax.ShapeDtypeStruct((256, W2), bf16),
        in_specs=[smem, smem] + [anyspace] * 5,
        out_specs=pl.BlockSpec(memory_space=pltpu.VMEM),
        scratch_shapes=scratch,
        compiler_params=pltpu.CompilerParams(
            collective_id=0, has_side_effects=True, vmem_limit_bytes=VMEM
        ),
        cost_estimate=pl.CostEstimate(
            flops=2 * 2048 * 4096 * 512, bytes_accessed=6 * 1024 * 1024, transcendentals=0
        ),
    )(task_ab, task_ef, w, lam_pairs, other_terms, vir_pair.reshape(2, 128), occ_pair.reshape(1, W2))


def solution(mesh):
    placed = (
        P(("col", "row"), None, None),
        P(("col", "row")),
        P(("col", "row")),
        P("row", "col"),
        P("row", "col"),
        P("row"),
        P("col"),
    )
    return jax.shard_map(
        body, mesh=mesh, in_specs=placed, out_specs=P("row", "col"), check_vma=False
    )
```

```python
import jax
import jax.numpy as jnp
from jax import lax
from jax.experimental import pallas as pl
from jax.experimental.pallas import tpu as pltpu
from jax.sharding import PartitionSpec as P

TILE = 512
AB_T = 4
EF_T = 8
NX = NY = 4
NZ = 8
NK = 8
R = 16
W2 = 512
VMEM = 54784 * 1024

S_1A, S_1B, S_2A, S_2B, S_MM, S_H1, S_H2, S_H3, S_FIN = range(9)


ORDER = (
     3,  5,  2,  1,  7,  4, 13,  0, 15,  6, 11, 12, 14, 23, 22, 21,
    24, 33, 31, 32, 34, 10, 25, 16, 43, 41, 17, 42, 20, 53, 44, 35,
    51, 52, 26, 63, 27, 54, 61, 45, 62, 73, 36, 30, 55, 64, 37, 71,
    72, 46, 40, 65, 47, 74, 56, 83, 82, 50, 57, 75, 66, 60, 67, 85,
    76, 70, 84, 77, 81, 80, 86, 87,
)
DIRECT = ()


def split(v):
    high = v.astype(jnp.bfloat16)
    wide = high.astype(jnp.float32)
    most = jnp.max(jnp.abs(wide), axis=0, keepdims=True)
    scale = jnp.where(most > 1e-33, 32512.0 / most, 0.0)
    u = ((v - wide) * scale + 128.5).astype(jnp.int32)
    low = u[:, 384:]
    for part, bits in ((u[:, :128], 24), (u[:, 128:256], 16), (u[:, 256:384], 8)):
        low = low | lax.shift_left(part, jnp.full(part.shape, bits, jnp.int32))
    return high, low


def join(high, low):
    wide = high.astype(jnp.float32)
    most = jnp.max(jnp.abs(wide), axis=0, keepdims=True)
    parts = [
        lax.shift_right_logical(low, jnp.full(low.shape, bits, jnp.int32)) & 255 for bits in (24, 16, 8)
    ] + [low & 255]
    u = jnp.concatenate(parts, axis=1)
    return wide + (u - 128).astype(jnp.float32) * (most * (1.0 / 32512.0))


def kernel(ab_ref, ef_ref, w_ref, lam_ref, other_ref, vir_ref, occ_ref, out_ref, *scratch):
    land = scratch[:NK]
    part = scratch[NK : 2 * NK]
    (
        w_v, lam_v, lhs, hop0, hop1, hop2, last, low0, low1, low2, lowl, out0, outs, lout0, louts, swap, other_v, vir_v, occ_v, vir_t,
        ids, inv_v, inv_s,
        in_sem, lam_send, lam_recv, id_send, id_recv, c_send, g_recv, h_recv, s_recv,
    ) = scratch[2 * NK :]

    col = lax.axis_index("col")
    z = lax.axis_index("row")
    core = lax.rem(col, 2)
    y = lax.rem(col // 2, NY)
    x = col // (2 * NY)

    def dev(xx, yy, cc, zz):
        return ((xx * NY + yy) * 2 + cc, zz)

    def step4(v, d):
        return lax.rem(v + (4 + d), 4)

    def stepz(v, d):
        return lax.rem(v + (NZ + d), NZ)

    def remote(src, dst, send, recv, device):
        return pltpu.make_async_remote_copy(
            src_ref=src, dst_ref=dst, send_sem=send, recv_sem=recv,
            device_id=device, device_id_type=pl.DeviceIdType.MESH,
        )

    partner = dev(x, y, 1 - core, z)
    prime = (x, y)
    second = (y, x)
    near = {
        (axis, d, j): dev(step4(x, d), y, j, z) if axis == 0 else dev(x, step4(y, d), j, z)
        for axis in (0, 1) for d in (1, -1, 2) for j in (0, 1)
    }

    def around(axis, d, j):
        if axis == 0:
            return dev(step4(x, d), y, j, z)
        return dev(x, step4(y, d), j, z)

    updown = {d: [dev(x, y, j, stepz(z, d)) for j in (0, 1)] for d in (1, -1)}

    get_w = pltpu.make_async_copy(w_ref, w_v, in_sem.at[0])
    get_w.start()
    get_lam = pltpu.make_async_copy(lam_ref, lam_v.at[core], in_sem.at[1])
    get_lam.start()
    small = [
        pltpu.make_async_copy(vir_ref, vir_v, in_sem.at[2]),
        pltpu.make_async_copy(occ_ref, occ_v, in_sem.at[3]),
        pltpu.make_async_copy(other_ref, other_v, in_sem.at[4]),
    ]
    for c in small:
        c.start()

    barrier = pltpu.get_barrier_semaphore()
    greeted = [partner] + list(near.values()) + updown[1] + updown[-1]
    for who in greeted:
        pl.semaphore_signal(barrier, inc=1, device_id=who, device_id_type=pl.DeviceIdType.MESH)

    my_slot = core * 16 + jnp.where(core == 0, y * 4 + x, x * 4 + y)
    my_id = (y * 4 + x) * 2 + core
    code = ab_ref[0] * EF_T + ef_ref[0]
    lane = lax.broadcasted_iota(jnp.int32, (1, 128), 1)
    ids[my_id] = jnp.where(lane == code, my_slot, 0)
    get_w.wait()
    for k in range(NK):
        land[k][my_slot] = w_v[:, core, k]

    pl.semaphore_wait(barrier, len(greeted))

    def mine_along(d, j):
        xx = jnp.where(core == 0, step4(x, d), x)
        yy = jnp.where(core == 0, y, step4(y, d))
        return dev(xx, yy, j, z)

    def stage_1a(k):
        send, recv = c_send.at[k], g_recv.at[k, 0]
        hops = (1, -1, 2) if k in DIRECT else (1, -1)
        for d in hops:
            for j in (0, 1):
                remote(w_v.at[:, j, k], land[k].at[my_slot], send, recv, mine_along(d, j)).start()
        remote(w_v.at[:, 1 - core, k], land[k].at[my_slot], send, recv, partner).start()
        expect(land[k].at[pl.ds(0, 2 * len(hops) + 1)], send, recv, (k, 0))

    arrivals = {}

    def expect(view, send, recv, key):
        arrivals[key] = remote(view, view, send, recv, partner)

    def slot(g, s, p):
        return g * 16 + s * 4 + p

    def stage_1b(k):
        arrivals[k, 0].wait_recv()
        send, recv = c_send.at[k], g_recv.at[k, 1]
        for g in (0, 1):
            for n, d in enumerate((1, -1)):
                view = land[k].at[slot(g, second[g], step4(prime[g], -d)), n]
                remote(view, view, send, recv, around(g, d, core)).start()
        expect(land[k].at[pl.ds(0, 2)], send, recv, (k, 1))

    def stage_2a(k):
        arrivals[k, 0 if k in DIRECT else 1].wait_recv()
        send, recv = c_send.at[k], g_recv.at[k, 2]
        hops = (1, -1, 2) if k in DIRECT else (1, -1)
        for g in (0, 1):
            view = land[k].at[pl.ds(slot(g, second[g], 0), 4)]
            for d in hops:
                remote(view, view, send, recv, around(1 - g, d, core)).start()
        expect(land[k].at[pl.ds(0, 8 * len(hops))], send, recv, (k, 2))

    def stage_2b(k):
        arrivals[k, 2].wait_recv()
        send, recv = c_send.at[k], g_recv.at[k, 3]
        for g in (0, 1):
            for n, d in enumerate((1, -1)):
                view = land[k].at[pl.ds(slot(g, step4(second[g], -d), 2 * n), 2)]
                remote(view, view, send, recv, around(1 - g, d, core)).start()
        expect(land[k].at[pl.ds(0, 8)], send, recv, (k, 3))

    def ids_first():
        for d in (1, -1, 2):
            for j in (0, 1):
                remote(ids.at[my_id], ids.at[my_id], id_send.at[0], id_recv.at[0], around(0, d, j)).start()
        remote(ids.at[my_id], ids.at[my_id], id_send.at[0], id_recv.at[0], partner).start()
        expect(ids.at[pl.ds(0, 7)], id_send.at[0], id_recv.at[0], "id0")

    def ids_second():
        arrivals["id0"].wait_recv()
        view = ids.at[pl.ds(y * 8, 8)]
        for d in (1, -1, 2):
            remote(view, view, id_send.at[1], id_recv.at[1], around(1, d, core)).start()
        expect(ids.at[pl.ds(0, 24)], id_send.at[1], id_recv.at[1], "id1")

    def ids_done():
        arrivals["id1"].wait_recv()
        inv_v[...] = jnp.max(ids[...], axis=0)
        get = pltpu.make_async_copy(inv_v, inv_s, in_sem.at[5])
        get.start()
        for c in small:
            c.wait()
        for n in (0, 1):
            row = jnp.broadcast_to(vir_v[n : n + 1, :], (128, 128))
            vir_t[n * 128 : (n + 1) * 128, :] = row.T
        get.wait()
        get_lam.wait()
        give_lam.wait_recv()

    def multiply(k):
        arrivals[k, 2 if k in DIRECT else 3].wait_recv()

        def order(ab, carry):
            for ef in range(EF_T):
                tile = land[k][inv_s[0, ab * EF_T + ef]]
                rows = pl.ds(pl.multiple_of(ab * (2 * R), 2 * R), 2 * R)
                lhs[rows, ef * TILE : (ef + 1) * TILE] = tile.reshape(2 * R, TILE)
            return carry

        lax.fori_loop(0, AB_T, order, 0)

        def half(j, carry):
            for q in range(W2 // 256):
                cols = slice(q * 256, (q + 1) * 256)
                product = jnp.dot(lhs[...], lam_v[j, :, cols], preferred_element_type=jnp.float32)
                part[k][j, :, :, cols] = product.reshape(NZ, R, 256)
            return carry

        lax.fori_loop(0, 2, half, 0)
        far = stepz(z, 4)
        for n, d in enumerate((1, -1)):
            out0[k, n], lout0[k, n] = split(part[k][n, far])
            ship(k, 0, out0.at[k, n], lout0.at[k, n], hop0.at[k, n], low0.at[k, n], near_z(d))
        expect_hop(k, 0)
        give = remote(part[k].at[1 - core, z], swap.at[k], c_send.at[k], s_recv.at[k], partner)
        give.start()
        arrivals[k, "swap"] = give

    def near_z(d):
        return dev(x, y, core, stepz(z, d))

    def ship(k, stage, high, low, high_to, low_to, who):
        remote(high, high_to, c_send.at[k], h_recv.at[k, stage], who).start()
        remote(low, low_to, c_send.at[k], h_recv.at[k, stage], who).start()

    def expect_hop(k, stage):
        expect(lam_v.at[0, pl.ds(0, 48 if stage == 0 else 96)], c_send.at[k], h_recv.at[k, stage], (k, "hop", stage))

    def arrived(k, stage):
        arrivals[k, "hop", stage].wait_recv()

    def hop_1(k):
        arrived(k, 0)
        for n, d in enumerate((1, -1)):
            block = stepz(z, 3 * d)
            for j in (0, 1):
                v = part[k][j, block]
                if j == n:
                    v = v + join(hop0[k, n], low0[k, n])
                outs[k, 0, n, j], louts[k, 0, n, j] = split(v)
            ship(k, 1, outs.at[k, 0, n], louts.at[k, 0, n], hop1.at[k, n], low1.at[k, n], near_z(d))
        expect_hop(k, 1)

    def hop_2(k):
        arrived(k, 1)
        for n, d in enumerate((1, -1)):
            block = stepz(z, 2 * d)
            for j in (0, 1):
                v = part[k][j, block] + join(hop1[k, n, j], low1[k, n, j])
                outs[k, 1, n, j], louts[k, 1, n, j] = split(v)
            ship(k, 2, outs.at[k, 1, n], louts.at[k, 1, n], hop2.at[k, n], low2.at[k, n], near_z(d))
        expect_hop(k, 2)

    def hop_3(k):
        arrived(k, 2)
        for n, d in enumerate((1, -1)):
            block = stepz(z, d)
            for j in (0, 1):
                v = part[k][j, block] + join(hop2[k, n, j], low2[k, n, j])
                outs[k, 2, n, j], louts[k, 2, n, j] = split(v)
                ship(
                    k, 3, outs.at[k, 2, n, j], louts.at[k, 2, n, j],
                    last.at[k, n, core], lowl.at[k, n, core], updown[d][j],
                )
        expect_hop(k, 3)

    def finish(k):
        arrivals[k, "swap"].wait_recv()
        arrived(k, 3)
        for who, own in ((core, part[k][core, z]), (1 - core, swap[k])):
            rows = pl.ds(pl.multiple_of(who * 128 + k * R, R), R)
            ladder = own + join(last[k, 0, who], lowl[k, 0, who]) + join(last[k, 1, who], lowl[k, 1, who])
            v = vir_t[rows, :]
            den = occ_v[...] - jnp.concatenate([v] * (W2 // 128), axis=1)
            out_ref[rows, :] = ((other_v[rows, :].astype(jnp.float32) + ladder) / den).astype(jnp.bfloat16)

    stage_1a(ORDER[0])
    ids_first()
    give_lam = remote(lam_ref, lam_v.at[core], lam_send, lam_recv, partner)

    run = (stage_1a, stage_1b, stage_2a, stage_2b, multiply, hop_1, hop_2, hop_3, finish)
    first_2a = next(n for n, item in enumerate(ORDER) if item // 10 == S_2A)
    first_mm = next(n for n, item in enumerate(ORDER) if item // 10 == S_MM)
    for n, item in enumerate(ORDER):
        if n == first_2a:
            ids_second()
            give_lam.start()
        if n == first_mm:
            ids_done()
        if n > 0:
            run[item // 10](item % 10)

    for key in ("id0", "id1"):
        arrivals[key].wait_send()
    give_lam.wait_send()
    for k in range(NK):
        first = 7 * 32 if k in DIRECT else 5 * 32
        plane = first + (24 * 32 if k in DIRECT else 64 + 512 + 256)
        view = lam_v.at[0, pl.ds(0, plane + 48 + 3 * 96 + 32)]
        remote(view, view, c_send.at[k], s_recv.at[k], partner).wait_send()


def body(w_tiles, task_ab, task_ef, lam_pairs, other_terms, vir_pair, occ_pair):
    w = w_tiles.reshape(2, 2, NK, R, TILE)
    anyspace = pl.BlockSpec(memory_space=pl.ANY)
    smem = pl.BlockSpec(memory_space=pltpu.SMEM)
    f32, bf16 = jnp.float32, jnp.bfloat16
    dma = pltpu.SemaphoreType.DMA
    scratch = [pltpu.VMEM((32, 2, R, TILE), bf16) for _ in range(NK)]
    scratch += [pltpu.VMEM((2, NZ, R, W2), f32) for _ in range(NK)]
    scratch += [
        pltpu.VMEM((2, 2, NK, R, TILE), bf16),
        pltpu.VMEM((2, EF_T * TILE, W2), bf16),
        pltpu.VMEM((AB_T * 2 * R, EF_T * TILE), bf16),
        pltpu.VMEM((NK, 2, R, W2), bf16),
        pltpu.VMEM((NK, 2, 2, R, W2), bf16),
        pltpu.VMEM((NK, 2, 2, R, W2), bf16),
        pltpu.VMEM((NK, 2, 2, R, W2), bf16),
        pltpu.VMEM((NK, 2, R, 128), jnp.int32),
        pltpu.VMEM((NK, 2, 2, R, 128), jnp.int32),
        pltpu.VMEM((NK, 2, 2, R, 128), jnp.int32),
        pltpu.VMEM((NK, 2, 2, R, 128), jnp.int32),
        pltpu.VMEM((NK, 2, R, W2), bf16),
        pltpu.VMEM((NK, 3, 2, 2, R, W2), bf16),
        pltpu.VMEM((NK, 2, R, 128), jnp.int32),
        pltpu.VMEM((NK, 3, 2, 2, R, 128), jnp.int32),
        pltpu.VMEM((NK, R, W2), f32),
        pltpu.VMEM((256, W2), bf16),
        pltpu.VMEM((2, 128), f32),
        pltpu.VMEM((1, W2), f32),
        pltpu.VMEM((256, 128), f32),
        pltpu.VMEM((32, 1, 128), jnp.int32),
        pltpu.VMEM((1, 128), jnp.int32),
        pltpu.SMEM((1, 128), jnp.int32),
        dma((6,)),
        dma, dma,
        dma((2,)), dma((2,)),
        dma((NK,)), dma((NK, 4)),
        dma((NK, 4)), dma((NK,)),
    ]
    return pl.pallas_call(
        kernel,
        out_shape=jax.ShapeDtypeStruct((256, W2), bf16),
        in_specs=[smem, smem] + [anyspace] * 5,
        out_specs=pl.BlockSpec(memory_space=pltpu.VMEM),
        scratch_shapes=scratch,
        compiler_params=pltpu.CompilerParams(
            collective_id=0, has_side_effects=True, vmem_limit_bytes=VMEM
        ),
        cost_estimate=pl.CostEstimate(
            flops=2 * 2048 * 4096 * 512, bytes_accessed=6 * 1024 * 1024, transcendentals=0
        ),
    )(task_ab, task_ef, w, lam_pairs, other_terms, vir_pair.reshape(2, 128), occ_pair.reshape(1, W2))


def solution(mesh):
    placed = (
        P(("col", "row"), None, None),
        P(("col", "row")),
        P(("col", "row")),
        P("row", "col"),
        P("row", "col"),
        P("row"),
        P("col"),
    )
    return jax.shard_map(
        body, mesh=mesh, in_specs=placed, out_specs=P("row", "col"), check_vma=False
    )
```
